1024 devices in a mesh: dp: 4 (over x), expert: 8 (over y, core), tensor: 32 (over z).
Axes of the slice: x: 4, y: 4, z: 32, core: 2. Of those that a mesh axis runs over, the one named last changes fastest.
Arguments:
- tokens: bfloat16 [2048, 4096], P(('dp', 'expert'), 'tensor'), may hold values from -6 to 6
- cotangent: bfloat16 [2048, 4096], P(('dp', 'expert'), 'tensor'), may hold values from -6 to 6
- routes: int32 [2048, 2], P(('dp', 'expert')), may hold values from 0 to 7, all different within a row; in each aligned block of 64 rows (0 to 63, 64 to 127, ...) at most 24 rows name the same one
- gates: float32 [2048, 2], P(('dp', 'expert')), may hold values from 0.2 to 1
- w_gate: bfloat16 [8, 4096, 12288], P('expert', None, 'tensor'), may hold values from -0.1875 to 0.1875
- w_up: bfloat16 [8, 4096, 12288], P('expert', None, 'tensor'), may hold values from -0.1875 to 0.1875
- w_down: bfloat16 [8, 12288, 4096], P('expert', 'tensor'), may hold values from -0.109375 to 0.109375
Outputs:
- mixed: bfloat16 [2048, 4096], P(('dp', 'expert'), 'tensor')
- grad_input: bfloat16 [2048, 4096], P(('dp', 'expert'), 'tensor')
The draws below stay inside these ranges and needn't reach their ends.
Inputs may be any that keep to these rules, and one draw needn't show every extreme that they name: `routes`: each token names 2 different experts. Within each aligned block of 64 tokens no expert is named by more than 24 tokens, and in some blocks one expert is named by exactly 24.
All inputs are finite; a program needn't handle non-finite values.
Results may differ from the reference program's by a relative error of at most 0.03.
Values may be sent and summed in bfloat16 or wider, within the bound.
A program may use at most 64 MiB of HBM per device.

```python
import math
import jax
import jax.numpy as jnp
import numpy as np
from jax import lax

D = 4096
FF = 12288
TOP = 2
TOK_DEV = 64
EXPERTS = 8
CAP = 24
TOKENS = 2048
N_DP = 4
N_EXPERT = 8
N_TENSOR = 32


def spiked(result, rng, source, target, parts, factor):
    owner, partner = [(jnp.arange(result.shape[dim]) // (result.shape[dim] // parts)).reshape([-1 if axis == dim else 1 for axis in range(result.ndim)]) for dim in (source, target)]
    chosen = jax.random.permutation(rng, parts)[partner]
    strong = (owner == chosen) | (owner == (partner + parts // 2) % parts)
    return jnp.where(strong, factor * result, result)


def block_scale(own_key, shape, shards, low, high):
    loudness, own = 1.0, jax.random.fold_in(own_key, 6)
    for axis_at, blocks in shards:
        steps = jnp.exp(jax.random.uniform(jax.random.fold_in(own, axis_at), (blocks,), jnp.float32, low / len(shards), high / len(shards)))
        loudness = loudness * jnp.repeat(steps, shape[axis_at] // blocks).reshape([-1 if axis == axis_at else 1 for axis in range(len(shape))])
    return loudness


def deal_out(stream_key, own, number, rows, count, top, reach, slope):
    order = jax.random.permutation(stream_key, count)
    crowded, usual = load_shares(count, rows * top, reach, slope, True), load_shares(count, rows * top, reach, slope, False)
    places = jnp.arange(count)

    def named(tallies, turn):
        used = int((tallies > 0).sum())
        fixed = max(1, used // 4)
        moved = fixed + (places - fixed + turn * (used - fixed)) % max(1, count - fixed)
        return jnp.zeros((count,), jnp.int32).at[order[jnp.where(places < fixed, places, moved)]].set(jnp.asarray(tallies, jnp.int32))

    tallies = jnp.where(number % 4 == 0, named(crowded, number // 4), named(usual, number - number // 4 - 1))
    mixed = jax.random.permutation(jax.random.fold_in(own, 3), count)
    giver, sink = mixed[0:count // 2 * 2:2], mixed[1:count // 2 * 2:2]
    slack = jnp.minimum(tallies[giver] - 1, reach - tallies[sink]) // 2
    slack = jnp.where((giver == order[0]) | (sink == order[0]) | (tallies[sink] == 0), 0, jnp.maximum(slack, 0))
    moved = jax.random.randint(jax.random.fold_in(own, 4), (count // 2,), 0, 1 << 20) % (slack + 1)
    tallies = tallies.at[giver].add(-moved).at[sink].add(moved)
    labels = jnp.searchsorted(jnp.cumsum(tallies), jnp.arange(rows * top), side="right").astype(jnp.int32)
    table = labels.reshape(top, rows).T
    table = table[jax.random.permutation(jax.random.fold_in(own, 1), rows)]
    turn = jax.random.randint(jax.random.fold_in(own, 2), (rows, 1), 0, top)
    return jnp.take_along_axis(table, (jnp.arange(top)[None, :] + turn) % top, axis=1)


def load_shares(amount, total, most, slope, full):
    portions = [(1 << 20) // math.isqrt(rank ** slope) + 1 for rank in range(1, amount + 1)]
    largest = most if full else min(most, max(-(-total // amount), total * portions[0] // sum(portions)))
    least = 1 if total - largest >= amount - 1 else 0
    given, spare = [largest] + [least] * (amount - 1), total - largest - least * (amount - 1)
    while spare > 0:
        free = [i for i in range(1, amount) if given[i] < largest] or [i for i in range(1, amount) if given[i] < most]
        mass, remaining = sum([portions[i] for i in free]), spare
        for i in free:
            addition = min(most - given[i], max(1, remaining * portions[i] // mass), spare)
            given[i] = given[i] + addition
            spare = spare - addition
    return np.array(given)


def scatter_about(key, shape, deviation, bound, split=(), held_as=jnp.bfloat16):
    array = deviation * jax.random.normal(key, shape, jnp.float32)
    if split:
        array = array * block_scale(key, shape, split, -0.22, 0.18)
    return jnp.clip(array, -bound, bound).astype(held_as)


def heavy_noise(stream_key, dims, scale, reach, shards, heavy, held_as=jnp.bfloat16):
    values = scale * jax.random.normal(stream_key, dims, jnp.float32)
    if shards:
        values = values * block_scale(stream_key, dims, shards, -0.22, 0.18)
    return jnp.clip(spiked(values, jax.random.fold_in(stream_key, 3), *heavy), -reach, reach).astype(held_as)


def setup_inputs(seed: int = 0) -> dict:
    seeds = jax.random.split(jax.random.key(seed), 8)
    tokens = scatter_about(seeds[0], (TOKENS, D), 1.0, 6.0, ((0, 32), (1, 32)))
    cotangent = scatter_about(seeds[1], (TOKENS, D), 1.0, 6.0, ((0, 32), (1, 32)))
    routes_keys = jax.random.split(jax.random.fold_in(seeds[2], 1), TOKENS // TOK_DEV)
    routes_turns = jax.random.permutation(jax.random.fold_in(seeds[2], 3), TOKENS // TOK_DEV)
    routes = jax.vmap(lambda own, number: deal_out(jax.random.fold_in(seeds[2], 2), own, number, TOK_DEV, EXPERTS, TOP, CAP, 2))(routes_keys, routes_turns).reshape((TOKENS, TOP))
    gates = jnp.clip(0.2 + 0.8 * jax.random.uniform(seeds[3], (TOKENS, TOP), jnp.float32) ** block_scale(seeds[3], (TOKENS, TOP), ((0, 32),), -0.2, 0.2), 0.2, 1.0)
    w_gate = heavy_noise(seeds[4], (EXPERTS, D, FF), D ** -0.5, 0.1875, ((0, 8), (2, 32)), (1, 2, 32, 2.75))
    w_up = heavy_noise(seeds[5], (EXPERTS, D, FF), D ** -0.5, 0.1875, ((0, 8), (2, 32)), (2, 1, 32, 2.75))
    w_down = heavy_noise(seeds[6], (EXPERTS, FF, D), FF ** -0.5, 0.109375, ((0, 8), (1, 32)), (1, 2, 32, 2.75))
    return {"tokens": tokens, "cotangent": cotangent, "routes": routes, "gates": gates, "w_gate": w_gate, "w_up": w_up, "w_down": w_down}


def reference(tokens, cotangent, routes, gates, w_gate, w_up, w_down):
    groups = N_DP * N_EXPERT
    assigned = TOK_DEV * TOP
    flat_routes = routes.reshape(groups, assigned)
    onehot = (flat_routes[:, :, None] == jnp.arange(EXPERTS, dtype=jnp.int32)[None, None, :]).astype(jnp.int32)
    running = jnp.cumsum(onehot, axis=1) - 1
    slot = jnp.sum(running * onehot, axis=2).astype(jnp.int32)
    slot_rows = (jnp.arange(groups, dtype=jnp.int32)[:, None] * CAP + slot).reshape(-1)
    expert_ids = flat_routes.reshape(-1)
    buffer_rows = groups * CAP
    token_rows = jnp.repeat(tokens, TOP, axis=0)
    weighted = (jnp.repeat(cotangent.astype(jnp.float32), TOP, axis=0) * gates.reshape(-1)[:, None]).astype(jnp.bfloat16)
    dispatched = jnp.zeros((EXPERTS, buffer_rows, D), jnp.bfloat16).at[expert_ids, slot_rows].set(token_rows)
    dispatched_grad = jnp.zeros((EXPERTS, buffer_rows, D), jnp.bfloat16).at[expert_ids, slot_rows].set(weighted)
    width = FF // N_TENSOR

    def expert_pass(inputs):
        rows_in, grads_in, gate_weight, up_weight, down_weight = inputs
        gate = jnp.dot(rows_in, gate_weight, preferred_element_type=jnp.float32)
        up = jnp.dot(rows_in, up_weight, preferred_element_type=jnp.float32)
        grad_hidden = lax.dot_general(grads_in, down_weight, (((1,), (1,)), ((), ())), preferred_element_type=jnp.float32)
        sigmoid_gate = jax.nn.sigmoid(gate)
        active = gate * sigmoid_gate
        hidden = (active * up).astype(jnp.bfloat16)
        grad_gate = (grad_hidden * up * sigmoid_gate * (1.0 + gate * (1.0 - sigmoid_gate))).astype(jnp.bfloat16)
        grad_up = (grad_hidden * active).astype(jnp.bfloat16)

        def add_block(carry, index):
            begin = index * width
            hidden_block = lax.dynamic_slice_in_dim(hidden, begin, width, 1)
            gate_block = lax.dynamic_slice_in_dim(grad_gate, begin, width, 1)
            up_block = lax.dynamic_slice_in_dim(grad_up, begin, width, 1)
            down_block = lax.dynamic_slice_in_dim(down_weight, begin, width, 0)
            wgate_block = lax.dynamic_slice_in_dim(gate_weight, begin, width, 1)
            wup_block = lax.dynamic_slice_in_dim(up_weight, begin, width, 1)
            out_term = jnp.dot(hidden_block, down_block, preferred_element_type=jnp.float32)
            grad_term = lax.dot_general(gate_block, wgate_block, (((1,), (1,)), ((), ())), preferred_element_type=jnp.float32)
            grad_term = grad_term + lax.dot_general(up_block, wup_block, (((1,), (1,)), ((), ())), preferred_element_type=jnp.float32)
            out_round = lax.optimization_barrier(out_term.astype(jnp.bfloat16))
            grad_round = lax.optimization_barrier(grad_term.astype(jnp.bfloat16))
            return (carry[0] + out_round.astype(jnp.float32), carry[1] + grad_round.astype(jnp.float32)), None

        zeros = jnp.zeros((buffer_rows, D), jnp.float32)
        totals, unused = lax.scan(add_block, (zeros, zeros), jnp.arange(N_TENSOR, dtype=jnp.int32))
        return totals[0].astype(jnp.bfloat16), totals[1].astype(jnp.bfloat16)

    expert_out, expert_grad = lax.map(expert_pass, (dispatched, dispatched_grad, w_gate, w_up, w_down))
    picked_out = expert_out[expert_ids, slot_rows].astype(jnp.float32).reshape(TOKENS, TOP, D)
    picked_grad = expert_grad[expert_ids, slot_rows].astype(jnp.float32).reshape(TOKENS, TOP, D)
    mixed = jnp.sum(picked_out * gates[:, :, None], axis=1).astype(jnp.bfloat16)
    grad_input = jnp.sum(picked_grad, axis=1).astype(jnp.bfloat16)
    return mixed, grad_input
```

```python
import functools

import jax
import jax.numpy as jnp
from jax import lax
from jax.experimental import pallas as pl
from jax.experimental.pallas import tpu as pltpu
from jax.sharding import PartitionSpec as P

MESH = pl.DeviceIdType.MESH
F32 = jnp.float32
BF16 = jnp.bfloat16
NT = (((1,), (1,)), ((), ()))


def kernel(
    cap,
    nz,
    tok_ref,
    cot_ref,
    routes_ref,
    gates_ref,
    wg_hbm,
    wu_hbm,
    wd_hbm,
    mixed_ref,
    grad_ref,
    wg,
    wu,
    wd,
    raw,
    stage,
    even,
    odd,
    acc,
    hid,
    gg,
    gu,
    qt_ref,
    gs_ref,
    pick_ref,
    odd_out,
    odd_in,
    back,
    home,
    chain_out,
    chain_in,
    w_sem,
    raw_s,
    raw_r,
    y_s,
    y_r,
    odd_s,
    odd_r,
    po_s,
    po_r,
    b_s,
    b_r,
    c_s,
    c_r,
):
    dp, me, z = lax.axis_index("dp"), lax.axis_index("expert"), lax.axis_index("tensor")
    ne = lax.axis_size("expert")
    toks, cols = tok_ref.shape
    hidden = wd.shape[0]
    pair = 2 * cap
    rows = ne * pair
    last = nz // 4

    def at_z(offset):
        return (dp, me, lax.rem(z + offset + nz, nz))

    def peer(i):
        return (dp, lax.rem(me + i, ne), z)

    def remote(src, dst, send, recv, device):
        return pltpu.make_async_remote_copy(
            src_ref=src, dst_ref=dst, send_sem=send, recv_sem=recv, device_id=device, device_id_type=MESH
        )

    def feat(offset):
        return pl.ds(pl.multiple_of(lax.rem(z + offset + nz, nz) * cols, cols), cols)

    loads = [
        pltpu.make_async_copy(src, dst, w_sem.at[i])
        for i, (src, dst) in enumerate(((wg_hbm.at[0], wg), (wu_hbm.at[0], wu), (wd_hbm.at[0], wd)))
    ]
    barrier = pltpu.get_barrier_semaphore()
    greeted = [at_z(1), at_z(-1), at_z(2), at_z(-2)] + [peer(i) for i in range(1, ne)]
    for device in greeted:
        pl.semaphore_signal(barrier, inc=1, device_id=device, device_id_type=MESH)
    for load in loads:
        load.start()

    raw[0, 0:toks, :] = tok_ref[...]
    raw[0, toks : 2 * toks, :] = cot_ref[...]
    lane = lax.broadcasted_iota(jnp.int32, (toks, 128), 1)
    chosen = [(routes_ref[:, k : k + 1] == lane).astype(F32) for k in range(2)]
    before = (
        lax.broadcasted_iota(jnp.int32, (toks, toks), 1) < lax.broadcasted_iota(jnp.int32, (toks, toks), 0)
    ).astype(BF16)
    counts = jnp.dot(before, (chosen[0] + chosen[1]).astype(BF16), preferred_element_type=F32)
    target = [
        jnp.sum(chosen[k] * (counts + (lane * pair).astype(F32)), axis=1, keepdims=True) for k in range(2)
    ]
    wide = lax.broadcasted_iota(jnp.int32, (toks, rows), 1).astype(F32)
    for k in range(2):
        pick_ref[k * toks : (k + 1) * toks, :] = (wide == target[k]).astype(BF16)
    pick_ref[2 * toks : 3 * toks, :] = (
        (wide == target[0] + cap).astype(F32) + (wide == target[1] + cap).astype(F32)
    ).astype(BF16)
    token = lax.broadcasted_iota(jnp.int32, (toks, 2 * toks), 0)
    column = lax.broadcasted_iota(jnp.int32, (toks, 2 * toks), 1)
    diagonal = (column == token) | (column == token + toks)
    down_rows = lax.broadcasted_iota(jnp.int32, (rows, 2 * toks), 0).astype(F32)
    lanes1 = lax.broadcasted_iota(jnp.int32, (1, 2 * toks), 1)
    second = jnp.where(lanes1 < toks, 0.0, float(cap))
    placing, scale = 0.0, 0.0
    for k in range(2):
        row_target = jnp.sum(jnp.where(diagonal, target[k], 0.0), axis=0, keepdims=True) + second
        row_gate = jnp.sum(jnp.where(diagonal, gates_ref[:, k : k + 1], 0.0), axis=0, keepdims=True)
        row_gate = jnp.where(lanes1 < toks, 1.0, row_gate)
        hit = down_rows == row_target
        placing = placing + hit.astype(F32)
        scale = scale + jnp.sum(jnp.where(hit, row_gate, 0.0), axis=1, keepdims=True)
    qt_ref[...] = placing.astype(BF16)
    gs_ref[...] = jnp.broadcast_to(scale, (rows, 128))

    pl.semaphore_wait(barrier, len(greeted))

    def raw_copy(k, d):
        src = raw.at[0] if isinstance(k, int) and k == 1 else raw.at[2 * k - 3 + d]
        i = 2 * k - 1 + d
        return remote(src, raw.at[i], raw_s.at[i], raw_r.at[i], at_z(2 - 4 * d))

    def raw_last(d):
        src = raw.at[2 * last - 3 + d, pl.ds(d * toks, toks)]
        dst = raw.at[2 * last - 1, pl.ds(d * toks, toks)]
        i = 2 * last - 1 + d
        return remote(src, dst, raw_s.at[i], raw_r.at[i], at_z(2 - 4 * d))

    def single(k):
        return isinstance(k, int) and k in (0, last)

    def first_slice(k):
        return 0 if isinstance(k, int) and k == 0 else 2 * k - 1

    def y_copy(k, i, out, into, send, recv):
        to = lax.rem(me + i, ne)
        if single(k):
            return remote(out.at[k, to, 0], into.at[first_slice(k), me], send.at[k, i], recv.at[k, i], peer(i))
        return remote(
            out.at[k, to], into.at[pl.ds(2 * k - 1, 2), me], send.at[k, i], recv.at[k, i], peer(i)
        )

    def slices(k):
        return 1 if single(k) else 2

    def exchange(k, out, into, send, recv):
        for i in range(1, ne):
            y_copy(k, i, out, into, send, recv).start()
        for d in range(slices(k)):
            into[first_slice(k) + d, me] = out[k, me, d]

    def dispatch(k):
        n = slices(k)
        block = raw[first_slice(k)]
        if n == 2:
            block = jnp.concatenate([block, raw[2 * k]], axis=1)
        placed = jnp.dot(qt_ref[...], block, preferred_element_type=F32)
        for d in range(n):
            one = (placed[:, d * cols : (d + 1) * cols] * gs_ref[...]).astype(BF16)
            stage[k, :, d] = one.reshape(ne, pair, cols)
        exchange(k, stage, even, y_s, y_r)

    def odd_copy(k, d):
        src = even.at[0] if isinstance(k, int) and k == 0 else even.at[2 * k - 1 + d]
        i = 2 * k + d
        return remote(src, odd.at[i], odd_s.at[i], odd_r.at[i], at_z(1 - 2 * d))

    def pass_on(k):
        for i in range(1, ne):
            y_copy(k, i, stage, even, y_s, y_r).wait_recv()
        if not (isinstance(k, int) and k == last):
            for d in range(2):
                odd_copy(k, d).start()

    def accumulate(parts, first=False):
        lhs = [buf[i].reshape(rows, cols) for buf, i, _ in parts]
        lhs = lhs[0] if len(lhs) == 1 else jnp.concatenate(lhs, axis=1)
        for n, w in enumerate((wg, wu, wd)):
            if n < 2:
                rhs = [w[feat(o), :] for _, _, o in parts]
                rhs = rhs[0] if len(rhs) == 1 else jnp.concatenate(rhs, axis=0)
                term = jnp.dot(lhs, rhs, preferred_element_type=F32)
            else:
                rhs = [w[:, feat(o)] for _, _, o in parts]
                rhs = rhs[0] if len(rhs) == 1 else jnp.concatenate(rhs, axis=1)
                term = lax.dot_general(lhs, rhs, NT, preferred_element_type=F32)
            span = slice(n * hidden, (n + 1) * hidden)
            if first:
                acc[:, span] = term
            else:
                acc[:, span] += term

    def even_parts(k):
        return [(even, 2 * k - 1, -2 * k), (even, 2 * k, 2 * k)]

    def odd_parts(k):
        return [(odd, 2 * k, -2 * k - 1), (odd, 2 * k + 1, 2 * k + 1)]

    def odd_arrived(k):
        for d in range(2):
            odd_copy(k, d).wait_recv()

    def y_sent(k, out, into, send, recv):
        for i in range(1, ne):
            y_copy(k, i, out, into, send, recv).wait_send()

    for d in range(2):
        raw_copy(1, d).start()
    dispatch(0)
    for d in range(2):
        raw_copy(1, d).wait_recv()
    for d in range(2):
        raw_copy(2, d).start()
    dispatch(1)
    pass_on(0)
    for load in loads:
        load.wait()
    accumulate([(even, 0, 0)], first=True)
    for d in range(2):
        raw_copy(1, d).wait_send()

    def gather_step(k, forward):
        for d in range(2):
            raw_copy(k, d).wait_recv()
        forward()
        dispatch(k)
        pass_on(k - 1)
        odd_arrived(k - 2)
        accumulate(even_parts(k - 1) + odd_parts(k - 2))
        for d in range(2):
            raw_copy(k, d).wait_send()
            odd_copy(k - 2, d).wait_send()
        y_sent(k - 2, stage, even, y_s, y_r)

    def forward_next(k):
        for d in range(2):
            raw_copy(k + 1, d).start()

    def forward_last():
        for d in range(2):
            raw_last(d).start()

    gather_step(2, lambda: forward_next(2))

    def gather_loop(k, carry):
        gather_step(k, lambda: forward_next(k))
        return carry

    lax.fori_loop(3, last - 1, gather_loop, 0)
    gather_step(last - 1, forward_last)
    for d in range(2):
        raw_last(d).wait_recv()
    dispatch(last)
    pass_on(last - 1)
    odd_arrived(last - 2)
    accumulate(even_parts(last - 1) + odd_parts(last - 2))
    pass_on(last)
    odd_arrived(last - 1)
    accumulate([(even, 2 * last - 1, 2 * last)] + odd_parts(last - 1))

    for j in range(ne // 2):
        top = 2 * pair * j
        mine = jnp.concatenate([acc[top : top + cap, :], acc[top + pair : top + pair + cap, :]], axis=0)
        gh = jnp.concatenate(
            [acc[top + cap : top + pair, 2 * hidden :], acc[top + pair + cap : top + 2 * pair, 2 * hidden :]],
            axis=0,
        )
        gate, up = mine[:, :hidden], mine[:, hidden : 2 * hidden]
        sigmoid = jax.nn.sigmoid(gate)
        active = gate * sigmoid
        span = slice(pair * j, pair * (j + 1))
        hid[span, :] = (active * up).astype(BF16)
        gg[span, :] = (gh * up * sigmoid * (1.0 + gate * (1.0 - sigmoid))).astype(BF16)
        gu[span, :] = (gh * active).astype(BF16)

    def partial(offsets):
        down = [wd[:, feat(o)] for o in offsets]
        gate = [wg[feat(o), :] for o in offsets]
        up = [wu[feat(o), :] for o in offsets]
        if len(offsets) > 1:
            down = jnp.concatenate(down, axis=1)
            gate, up = jnp.concatenate(gate, axis=0), jnp.concatenate(up, axis=0)
        else:
            down, gate, up = down[0], gate[0], up[0]
        out = jnp.dot(hid[...], down, preferred_element_type=F32)
        grad = lax.dot_general(gg[...], gate, NT, preferred_element_type=F32)
        grad = grad + lax.dot_general(gu[...], up, NT, preferred_element_type=F32)
        parts = []
        for j in range(ne):
            parts += [out[cap * j : cap * (j + 1)], grad[cap * j : cap * (j + 1)]]
        return jnp.concatenate(parts, axis=0)

    def po_copy(k, d):
        i = 2 * k + d
        return remote(odd_out.at[i], odd_in.at[i], po_s.at[i], po_r.at[i], at_z(2 * d - 1))

    def send_odd(k):
        both = partial([-2 * k - 1, 2 * k + 1]).astype(BF16)
        for d in range(2):
            odd_out[2 * k + d] = both[:, d * cols : (d + 1) * cols]
            po_copy(k, d).start()

    def send_even(k):
        if isinstance(k, int) and k == last:
            total = [partial([2 * k])]
        elif isinstance(k, int) and k == 0:
            total = partial([0])
            for d in range(2):
                po_copy(0, d).wait_recv()
                total = total + odd_in[d].astype(F32)
            total = [total]
        else:
            both = partial([-2 * k, 2 * k])
            total = []
            for d in range(2):
                po_copy(k, d).wait_recv()
                total.append(both[:, d * cols : (d + 1) * cols] + odd_in[2 * k + d].astype(F32))
        for d in range(slices(k)):
            back[k, :, d] = total[d].astype(BF16).reshape(ne, pair, cols)
        exchange(k, back, home, b_s, b_r)

    def combine(k):
        for i in range(1, ne):
            y_copy(k, i, back, home, b_s, b_r).wait_recv()
        block = home[first_slice(k)].reshape(rows, cols)
        if slices(k) == 2:
            block = jnp.concatenate([block, home[2 * k].reshape(rows, cols)], axis=1)
        picked = jnp.dot(pick_ref[...], block, preferred_element_type=F32)
        mixed = gates_ref[:, 0:1] * picked[:toks] + gates_ref[:, 1:2] * picked[toks : 2 * toks]
        return mixed, picked[2 * toks :]

    def chain_copy(k, d):
        i = 2 * k - 2 + d
        return remote(
            chain_out.at[2 * k - 1 + d], chain_in.at[i], c_s.at[i], c_r.at[i], at_z(4 * d - 2)
        )

    def chain_first(d):
        i = 2 * last - 2 + d
        part = pl.ds(d * toks, toks)
        return remote(
            chain_out.at[2 * last - 1, part], chain_in.at[i, part], c_s.at[i], c_r.at[i], at_z(4 * d - 2)
        )

    def chain_step(k, halves=False):
        mixed, grad = combine(k)
        for d in range(2):
            span = slice(d * cols, (d + 1) * cols)
            i = 2 * k + d
            if halves:
                chain_first(d).wait_recv()
            else:
                chain_copy(k + 1, d).wait_recv()
            m, g = mixed[:, span], grad[:, span]
            if not halves or d == 0:
                m = m + chain_in[i, 0:toks, :].astype(F32)
            if not halves or d == 1:
                g = g + chain_in[i, toks : 2 * toks, :].astype(F32)
            chain_out[2 * k - 1 + d, 0:toks, :] = m.astype(BF16)
            chain_out[2 * k - 1 + d, toks : 2 * toks, :] = g.astype(BF16)
            chain_copy(k, d).start()

    send_odd(last - 1)
    send_even(last)
    send_odd(last - 2)
    send_even(last - 1)
    for d in range(2):
        raw_last(d).wait_send()
        odd_copy(last - 2, d).wait_send()
        odd_copy(last - 1, d).wait_send()
    for k in (last - 2, last - 1, last):
        y_sent(k, stage, even, y_s, y_r)
    mixed, grad = combine(last)
    chain_out[2 * last - 1, 0:toks, :] = mixed.astype(BF16)
    chain_out[2 * last - 1, toks : 2 * toks, :] = grad.astype(BF16)
    for d in range(2):
        chain_first(d).start()

    send_odd(last - 3)
    send_even(last - 2)
    chain_step(last - 1, halves=True)

    def back_loop(n, carry):
        k = last - 3 - n
        send_odd(k - 1)
        send_even(k)
        chain_step(k + 1)
        for d in range(2):
            po_copy(k + 2, d).wait_send()
            chain_copy(k + 2, d).wait_send()
        y_sent(k + 2, back, home, b_s, b_r)
        return carry

    lax.fori_loop(0, last - 3, back_loop, 0)
    send_even(0)
    chain_step(1)
    mixed, grad = combine(0)
    for d in range(2):
        chain_copy(1, d).wait_recv()
        mixed = mixed + chain_in[d, 0:toks, :].astype(F32)
        grad = grad + chain_in[d, toks : 2 * toks, :].astype(F32)
    mixed_ref[...] = mixed.astype(BF16)
    grad_ref[...] = grad.astype(BF16)
    for d in range(2):
        chain_first(d).wait_send()
        for k in (2, 1):
            chain_copy(k, d).wait_send()
        for k in (2, 1, 0):
            po_copy(k, d).wait_send()
    for k in (last, 2, 1, 0):
        y_sent(k, back, home, b_s, b_r)


def shards(tokens, cotangent, routes, gates, w_gate, w_up, w_down):
    ne, nz = lax.axis_size("expert"), lax.axis_size("tensor")
    toks, cols = tokens.shape
    width, hidden = w_gate.shape[1:]
    cap = toks * routes.shape[1] * 3 // (2 * ne)
    pair = 2 * cap
    rows = ne * pair
    steps = nz // 4 + 1
    half = nz // 2
    vmem = pl.BlockSpec(memory_space=pltpu.VMEM)
    anywhere = pl.BlockSpec(memory_space=pl.ANY)
    dma = pltpu.SemaphoreType.DMA
    out = jax.ShapeDtypeStruct((toks, cols), BF16)
    slab = pltpu.VMEM((half, ne, pair, cols), BF16)
    flat = pltpu.VMEM((half, rows, cols), BF16)
    staged = pltpu.VMEM((steps, ne, 2, pair, cols), BF16)
    return pl.pallas_call(
        functools.partial(kernel, cap, nz),
        out_shape=(out, out),
        in_specs=[vmem] * 4 + [anywhere] * 3,
        out_specs=(vmem, vmem),
        scratch_shapes=[
            pltpu.VMEM((width, hidden), BF16),
            pltpu.VMEM((width, hidden), BF16),
            pltpu.VMEM((hidden, width), BF16),
            pltpu.VMEM((half, 2 * toks, cols), BF16),
            staged,
            slab,
            slab,
            pltpu.VMEM((rows, 3 * hidden), F32),
            pltpu.VMEM((rows // 2, hidden), BF16),
            pltpu.VMEM((rows // 2, hidden), BF16),
            pltpu.VMEM((rows // 2, hidden), BF16),
            pltpu.VMEM((rows, 2 * toks), BF16),
            pltpu.VMEM((rows, 128), F32),
            pltpu.VMEM((3 * toks, rows), BF16),
            flat,
            flat,
            staged,
            slab,
            pltpu.VMEM((half, 2 * toks, cols), BF16),
            pltpu.VMEM((half, 2 * toks, cols), BF16),
            dma((3,)),
            dma((half + 1,)),
            dma((half + 1,)),
            dma((steps, ne)),
            dma((steps, ne)),
            dma((half,)),
            dma((half,)),
            dma((half,)),
            dma((half,)),
            dma((steps, ne)),
            dma((steps, ne)),
            dma((half,)),
            dma((half,)),
        ],
        name="moe_layer",
        cost_estimate=pl.CostEstimate(
            flops=12 * rows * width * hidden, bytes_accessed=6 * width * hidden, transcendentals=rows * hidden
        ),
        compiler_params=pltpu.CompilerParams(
            collective_id=0, has_side_effects=True, vmem_limit_bytes=48 * 1024 * 1024
        ),
    )(tokens, cotangent, routes, gates, w_gate, w_up, w_down)


def solution(mesh):
    return jax.shard_map(
        shards,
        mesh=mesh,
        in_specs=(
            P(("dp", "expert"), "tensor"),
            P(("dp", "expert"), "tensor"),
            P(("dp", "expert"), None),
            P(("dp", "expert"), None),
            P("expert", None, "tensor"),
            P("expert", None, "tensor"),
            P("expert", "tensor", None),
        ),
        out_specs=(P(("dp", "expert"), "tensor"), P(("dp", "expert"), "tensor")),
        check_vma=False,
    )
```

```python
import functools

import jax
import jax.numpy as jnp
from jax import lax
from jax.experimental import pallas as pl
from jax.experimental.pallas import tpu as pltpu
from jax.sharding import PartitionSpec as P

MESH = pl.DeviceIdType.MESH
F32 = jnp.float32
BF16 = jnp.bfloat16
NT = (((1,), (1,)), ((), ()))


def kernel(
    cap,
    nz,
    tok_hbm,
    cot_hbm,
    routes_hbm,
    gates_hbm,
    wg_hbm,
    wu_hbm,
    wd_hbm,
    mixed_ref,
    grad_ref,
    wg,
    wu,
    wd,
    raw,
    stage,
    even,
    odd,
    acc,
    hid,
    gg,
    gu,
    qt_ref,
    gs_ref,
    pick_ref,
    routes_ref,
    gates_ref,
    gate_cols,
    odd_out,
    odd_in,
    back,
    home,
    chain_out,
    chain_in,
    w_sem,
    raw_s,
    raw_r,
    y_s,
    y_r,
    odd_s,
    odd_r,
    po_s,
    po_r,
    b_s,
    b_r,
    c_s,
    c_r,
):
    dp, me, z = lax.axis_index("dp"), lax.axis_index("expert"), lax.axis_index("tensor")
    ne = lax.axis_size("expert")
    toks, cols = tok_hbm.shape
    hidden = wd.shape[0]
    pair = 2 * cap
    rows = ne * pair
    last = nz // 4

    def at_z(offset):
        return (dp, me, lax.rem(z + offset + nz, nz))

    def peer(i):
        return (dp, lax.rem(me + i, ne), z)

    def remote(src, dst, send, recv, device):
        return pltpu.make_async_remote_copy(
            src_ref=src, dst_ref=dst, send_sem=send, recv_sem=recv, device_id=device, device_id_type=MESH
        )

    def feat(offset):
        return pl.ds(pl.multiple_of(lax.rem(z + offset + nz, nz) * cols, cols), cols)

    loads = [
        pltpu.make_async_copy(src, dst, w_sem.at[i])
        for i, (src, dst) in enumerate(((wg_hbm.at[0], wg), (wu_hbm.at[0], wu), (wd_hbm.at[0], wd)))
    ]
    barrier = pltpu.get_barrier_semaphore()
    greeted = [at_z(1), at_z(-1), at_z(2), at_z(-2)] + [peer(i) for i in range(1, ne)]
    for device in greeted:
        pl.semaphore_signal(barrier, inc=1, device_id=device, device_id_type=MESH)
    small = [
        pltpu.make_async_copy(src, dst, w_sem.at[3 + i])
        for i, (src, dst) in enumerate(
            (
                (routes_hbm, routes_ref),
                (gates_hbm, gates_ref),
                (tok_hbm, raw.at[0, pl.ds(0, toks)]),
                (cot_hbm, raw.at[0, pl.ds(toks, toks)]),
            )
        )
    ]
    for load in small + loads:
        load.start()
    for load in small:
        load.wait()

    square = lax.broadcasted_iota(jnp.int32, (toks, toks), 0) == lax.broadcasted_iota(
        jnp.int32, (toks, toks), 1
    )

    def column_of(ref, k):
        return jnp.sum(jnp.where(square, ref[k : k + 1, :].astype(F32), 0.0), axis=1, keepdims=True)

    gate_col = [column_of(gates_ref, k) for k in range(2)]
    route_col = [column_of(routes_ref, k) for k in range(2)]
    for k in range(2):
        gate_cols[k] = jnp.broadcast_to(gate_col[k], (toks, cols))
    lane = lax.broadcasted_iota(jnp.int32, (toks, 128), 1)
    chosen = [(route_col[k] == lane.astype(F32)).astype(F32) for k in range(2)]
    before = (
        lax.broadcasted_iota(jnp.int32, (toks, toks), 1) < lax.broadcasted_iota(jnp.int32, (toks, toks), 0)
    ).astype(BF16)
    counts = jnp.dot(before, (chosen[0] + chosen[1]).astype(BF16), preferred_element_type=F32)
    target = [
        jnp.sum(chosen[k] * (counts + (lane * pair).astype(F32)), axis=1, keepdims=True) for k in range(2)
    ]
    wide = lax.broadcasted_iota(jnp.int32, (toks, rows), 1).astype(F32)
    for k in range(2):
        pick_ref[k * toks : (k + 1) * toks, :] = (wide == target[k]).astype(BF16)
    pick_ref[2 * toks : 3 * toks, :] = (
        (wide == target[0] + cap).astype(F32) + (wide == target[1] + cap).astype(F32)
    ).astype(BF16)
    token = lax.broadcasted_iota(jnp.int32, (toks, 2 * toks), 0)
    column = lax.broadcasted_iota(jnp.int32, (toks, 2 * toks), 1)
    diagonal = (column == token) | (column == token + toks)
    down_rows = lax.broadcasted_iota(jnp.int32, (rows, 2 * toks), 0).astype(F32)
    lanes1 = lax.broadcasted_iota(jnp.int32, (1, 2 * toks), 1)
    second = jnp.where(lanes1 < toks, 0.0, float(cap))
    placing, scale = 0.0, 0.0
    for k in range(2):
        row_target = jnp.sum(jnp.where(diagonal, target[k], 0.0), axis=0, keepdims=True) + second
        row_gate = jnp.sum(jnp.where(diagonal, gate_col[k], 0.0), axis=0, keepdims=True)
        row_gate = jnp.where(lanes1 < toks, 1.0, row_gate)
        hit = down_rows == row_target
        placing = placing + hit.astype(F32)
        scale = scale + jnp.sum(jnp.where(hit, row_gate, 0.0), axis=1, keepdims=True)
    qt_ref[...] = placing.astype(BF16)
    gs_ref[...] = jnp.broadcast_to(scale, (rows, 128))

    pl.semaphore_wait(barrier, len(greeted))

    def raw_copy(k, d):
        src = raw.at[0] if isinstance(k, int) and k == 1 else raw.at[2 * k - 3 + d]
        i = 2 * k - 1 + d
        return remote(src, raw.at[i], raw_s.at[i], raw_r.at[i], at_z(2 - 4 * d))

    def raw_last(d):
        src = raw.at[2 * last - 3 + d, pl.ds(d * toks, toks)]
        dst = raw.at[2 * last - 1, pl.ds(d * toks, toks)]
        i = 2 * last - 1 + d
        return remote(src, dst, raw_s.at[i], raw_r.at[i], at_z(2 - 4 * d))

    def single(k):
        return isinstance(k, int) and k in (0, last)

    def first_slice(k):
        return 0 if isinstance(k, int) and k == 0 else 2 * k - 1

    def y_copy(k, i, out, into, send, recv):
        to = lax.rem(me + i, ne)
        if single(k):
            return remote(out.at[k, to, 0], into.at[first_slice(k), me], send.at[k, i], recv.at[k, i], peer(i))
        return remote(
            out.at[k, to], into.at[pl.ds(2 * k - 1, 2), me], send.at[k, i], recv.at[k, i], peer(i)
        )

    def slices(k):
        return 1 if single(k) else 2

    def exchange(k, out, into, send, recv):
        for i in range(1, ne):
            y_copy(k, i, out, into, send, recv).start()
        for d in range(slices(k)):
            into[first_slice(k) + d, me] = out[k, me, d]

    def dispatch(k):
        n = slices(k)
        block = raw[first_slice(k)]
        if n == 2:
            block = jnp.concatenate([block, raw[2 * k]], axis=1)
        placed = jnp.dot(qt_ref[...], block, preferred_element_type=F32)
        for d in range(n):
            one = (placed[:, d * cols : (d + 1) * cols] * gs_ref[...]).astype(BF16)
            stage[k, :, d] = one.reshape(ne, pair, cols)
        exchange(k, stage, even, y_s, y_r)

    def odd_copy(k, d):
        src = even.at[0] if isinstance(k, int) and k == 0 else even.at[2 * k - 1 + d]
        i = 2 * k + d
        return remote(src, odd.at[i], odd_s.at[i], odd_r.at[i], at_z(1 - 2 * d))

    def pass_on(k):
        for i in range(1, ne):
            y_copy(k, i, stage, even, y_s, y_r).wait_recv()
        if not (isinstance(k, int) and k == last):
            for d in range(2):
                odd_copy(k, d).start()

    def accumulate(parts, first=False):
        lhs = [buf[i].reshape(rows, cols) for buf, i, _ in parts]
        lhs = lhs[0] if len(lhs) == 1 else jnp.concatenate(lhs, axis=1)
        for n, w in enumerate((wg, wu, wd)):
            if n < 2:
                rhs = [w[feat(o), :] for _, _, o in parts]
                rhs = rhs[0] if len(rhs) == 1 else jnp.concatenate(rhs, axis=0)
                term = jnp.dot(lhs, rhs, preferred_element_type=F32)
            else:
                rhs = [w[:, feat(o)] for _, _, o in parts]
                rhs = rhs[0] if len(rhs) == 1 else jnp.concatenate(rhs, axis=1)
                term = lax.dot_general(lhs, rhs, NT, preferred_element_type=F32)
            span = slice(n * hidden, (n + 1) * hidden)
            if first:
                acc[:, span] = term
            else:
                acc[:, span] += term

    def even_parts(k):
        return [(even, 2 * k - 1, -2 * k), (even, 2 * k, 2 * k)]

    def odd_parts(k):
        return [(odd, 2 * k, -2 * k - 1), (odd, 2 * k + 1, 2 * k + 1)]

    def odd_arrived(k):
        for d in range(2):
            odd_copy(k, d).wait_recv()

    def y_sent(k, out, into, send, recv):
        for i in range(1, ne):
            y_copy(k, i, out, into, send, recv).wait_send()

    def forward_next(k):
        for d in range(2):
            raw_copy(k + 1, d).start()

    def forward_last():
        for d in range(2):
            raw_last(d).start()

    def gather_step(k, forward):
        for d in range(2):
            raw_copy(k, d).wait_recv()
        forward()
        dispatch(k)
        for d in range(2):
            raw_copy(k, d).wait_send()

    def settle(k):
        for d in range(2):
            odd_copy(k, d).wait_send()
        y_sent(k, stage, even, y_s, y_r)

    for d in range(2):
        raw_copy(1, d).start()
    dispatch(0)
    gather_step(1, lambda: forward_next(1))
    gather_step(2, lambda: forward_next(2))
    pass_on(0)
    for load in loads:
        load.wait()
    accumulate([(even, 0, 0)], first=True)
    gather_step(3, lambda: forward_next(3))
    pass_on(1)
    accumulate(even_parts(1))

    def gather_full(k):
        gather_step(k, lambda: forward_next(k))
        pass_on(k - 2)
        odd_arrived(k - 4)
        accumulate(even_parts(k - 2) + odd_parts(k - 4))
        settle(k - 4)

    def gather_loop(k, carry):
        gather_full(k)
        return carry

    gather_full(4)
    lax.fori_loop(5, last - 1, gather_loop, 0)
    gather_step(last - 1, forward_last)
    pass_on(last - 3)
    odd_arrived(last - 5)
    accumulate(even_parts(last - 3) + odd_parts(last - 5))
    for d in range(2):
        raw_last(d).wait_recv()
    dispatch(last)
    pass_on(last - 2)
    odd_arrived(last - 4)
    accumulate(even_parts(last - 2) + odd_parts(last - 4))
    pass_on(last - 1)
    odd_arrived(last - 3)
    accumulate(even_parts(last - 1) + odd_parts(last - 3))
    pass_on(last)
    odd_arrived(last - 2)
    accumulate([(even, 2 * last - 1, 2 * last)] + odd_parts(last - 2))
    odd_arrived(last - 1)
    accumulate(odd_parts(last - 1))

    for j in range(ne // 2):
        top = 2 * pair * j
        mine = jnp.concatenate([acc[top : top + cap, :], acc[top + pair : top + pair + cap, :]], axis=0)
        gh = jnp.concatenate(
            [acc[top + cap : top + pair, 2 * hidden :], acc[top + pair + cap : top + 2 * pair, 2 * hidden :]],
            axis=0,
        )
        gate, up = mine[:, :hidden], mine[:, hidden : 2 * hidden]
        sigmoid = jax.nn.sigmoid(gate)
        active = gate * sigmoid
        span = slice(pair * j, pair * (j + 1))
        hid[span, :] = (active * up).astype(BF16)
        gg[span, :] = (gh * up * sigmoid * (1.0 + gate * (1.0 - sigmoid))).astype(BF16)
        gu[span, :] = (gh * active).astype(BF16)

    def partial(offsets):
        down = [wd[:, feat(o)] for o in offsets]
        gate = [wg[feat(o), :] for o in offsets]
        up = [wu[feat(o), :] for o in offsets]
        if len(offsets) > 1:
            down = jnp.concatenate(down, axis=1)
            gate, up = jnp.concatenate(gate, axis=0), jnp.concatenate(up, axis=0)
        else:
            down, gate, up = down[0], gate[0], up[0]
        out = jnp.dot(hid[...], down, preferred_element_type=F32)
        grad = lax.dot_general(gg[...], gate, NT, preferred_element_type=F32)
        grad = grad + lax.dot_general(gu[...], up, NT, preferred_element_type=F32)
        parts = []
        for j in range(ne):
            parts += [out[cap * j : cap * (j + 1)], grad[cap * j : cap * (j + 1)]]
        return jnp.concatenate(parts, axis=0)

    def po_copy(k, d):
        i = 2 * k + d
        return remote(odd_out.at[i], odd_in.at[i], po_s.at[i], po_r.at[i], at_z(2 * d - 1))

    def send_odd(k):
        both = partial([-2 * k - 1, 2 * k + 1]).astype(BF16)
        for d in range(2):
            odd_out[2 * k + d] = both[:, d * cols : (d + 1) * cols]
            po_copy(k, d).start()

    def send_even(k):
        if isinstance(k, int) and k == last:
            total = [partial([2 * k])]
        elif isinstance(k, int) and k == 0:
            total = partial([0])
            for d in range(2):
                po_copy(0, d).wait_recv()
                total = total + odd_in[d].astype(F32)
            total = [total]
        else:
            both = partial([-2 * k, 2 * k])
            total = []
            for d in range(2):
                po_copy(k, d).wait_recv()
                total.append(both[:, d * cols : (d + 1) * cols] + odd_in[2 * k + d].astype(F32))
        for d in range(slices(k)):
            back[k, :, d] = total[d].astype(BF16).reshape(ne, pair, cols)
        exchange(k, back, home, b_s, b_r)

    def combine(k):
        for i in range(1, ne):
            y_copy(k, i, back, home, b_s, b_r).wait_recv()
        block = home[first_slice(k)].reshape(rows, cols)
        if slices(k) == 2:
            block = jnp.concatenate([block, home[2 * k].reshape(rows, cols)], axis=1)
        picked = jnp.dot(pick_ref[...], block, preferred_element_type=F32)
        g0, g1 = gate_cols[0], gate_cols[1]
        if slices(k) == 2:
            g0, g1 = jnp.concatenate([g0, g0], axis=1), jnp.concatenate([g1, g1], axis=1)
        mixed = g0 * picked[:toks] + g1 * picked[toks : 2 * toks]
        return mixed, picked[2 * toks :]

    def chain_copy(k, d):
        i = 2 * k - 2 + d
        return remote(
            chain_out.at[2 * k - 1 + d], chain_in.at[i], c_s.at[i], c_r.at[i], at_z(4 * d - 2)
        )

    def chain_first(d):
        i = 2 * last - 2 + d
        part = pl.ds(d * toks, toks)
        return remote(
            chain_out.at[2 * last - 1, part], chain_in.at[i, part], c_s.at[i], c_r.at[i], at_z(4 * d - 2)
        )

    def chain_step(k, halves=False):
        mixed, grad = combine(k)
        for d in range(2):
            span = slice(d * cols, (d + 1) * cols)
            i = 2 * k + d
            if halves:
                chain_first(d).wait_recv()
            else:
                chain_copy(k + 1, d).wait_recv()
            m, g = mixed[:, span], grad[:, span]
            if not halves or d == 0:
                m = m + chain_in[i, 0:toks, :].astype(F32)
            if not halves or d == 1:
                g = g + chain_in[i, toks : 2 * toks, :].astype(F32)
            chain_out[2 * k - 1 + d, 0:toks, :] = m.astype(BF16)
            chain_out[2 * k - 1 + d, toks : 2 * toks, :] = g.astype(BF16)
            chain_copy(k, d).start()

    send_odd(last - 1)
    send_even(last)
    send_odd(last - 2)
    send_even(last - 1)
    send_odd(last - 3)
    send_odd(last - 4)
    send_even(last - 2)
    for d in range(2):
        raw_last(d).wait_send()
    for k in range(last - 5, last):
        settle(k)
    y_sent(last, stage, even, y_s, y_r)
    mixed, grad = combine(last)
    chain_out[2 * last - 1, 0:toks, :] = mixed.astype(BF16)
    chain_out[2 * last - 1, toks : 2 * toks, :] = grad.astype(BF16)
    for d in range(2):
        chain_first(d).start()
    chain_step(last - 1, halves=True)
    send_odd(last - 5)
    send_even(last - 3)

    def back_loop(n, carry):
        k = last - 2 - n
        chain_step(k)
        send_odd(k - 4)
        send_even(k - 2)
        for d in range(2):
            po_copy(k + 1, d).wait_send()
            chain_copy(k + 1, d).wait_send()
        y_sent(k + 1, back, home, b_s, b_r)
        return carry

    lax.fori_loop(0, last - 5, back_loop, 0)
    chain_step(3)
    send_even(1)
    chain_step(2)
    send_even(0)
    chain_step(1)
    mixed, grad = combine(0)
    for d in range(2):
        chain_copy(1, d).wait_recv()
        mixed = mixed + chain_in[d, 0:toks, :].astype(F32)
        grad = grad + chain_in[d, toks : 2 * toks, :].astype(F32)
    mixed_ref[...] = mixed.astype(BF16)
    grad_ref[...] = grad.astype(BF16)
    for d in range(2):
        chain_first(d).wait_send()
        for k in (4, 3, 2, 1):
            chain_copy(k, d).wait_send()
        for k in (4, 3, 2, 1, 0):
            po_copy(k, d).wait_send()
    for k in (last, 4, 3, 2, 1, 0):
        y_sent(k, back, home, b_s, b_r)


def shards(tokens, cotangent, routes, gates, w_gate, w_up, w_down):
    ne, nz = lax.axis_size("expert"), lax.axis_size("tensor")
    toks, cols = tokens.shape
    width, hidden = w_gate.shape[1:]
    cap = toks * routes.shape[1] * 3 // (2 * ne)
    pair = 2 * cap
    rows = ne * pair
    steps = nz // 4 + 1
    half = nz // 2
    vmem = pl.BlockSpec(memory_space=pltpu.VMEM)
    anywhere = pl.BlockSpec(memory_space=pl.ANY)
    dma = pltpu.SemaphoreType.DMA
    out = jax.ShapeDtypeStruct((toks, cols), BF16)
    slab = pltpu.VMEM((half, ne, pair, cols), BF16)
    flat = pltpu.VMEM((half, rows, cols), BF16)
    staged = pltpu.VMEM((steps, ne, 2, pair, cols), BF16)
    return pl.pallas_call(
        functools.partial(kernel, cap, nz),
        out_shape=(out, out),
        in_specs=[anywhere] * 7,
        out_specs=(vmem, vmem),
        scratch_shapes=[
            pltpu.VMEM((width, hidden), BF16),
            pltpu.VMEM((width, hidden), BF16),
            pltpu.VMEM((hidden, width), BF16),
            pltpu.VMEM((half, 2 * toks, cols), BF16),
            staged,
            slab,
            slab,
            pltpu.VMEM((rows, 3 * hidden), F32),
            pltpu.VMEM((rows // 2, hidden), BF16),
            pltpu.VMEM((rows // 2, hidden), BF16),
            pltpu.VMEM((rows // 2, hidden), BF16),
            pltpu.VMEM((rows, 2 * toks), BF16),
            pltpu.VMEM((rows, 128), F32),
            pltpu.VMEM((3 * toks, rows), BF16),
            pltpu.VMEM((2, toks), jnp.int32),
            pltpu.VMEM((2, toks), F32),
            pltpu.VMEM((2, toks, cols), F32),
            flat,
            flat,
            staged,
            slab,
            pltpu.VMEM((half, 2 * toks, cols), BF16),
            pltpu.VMEM((half, 2 * toks, cols), BF16),
            dma((7,)),
            dma((half + 1,)),
            dma((half + 1,)),
            dma((steps, ne)),
            dma((steps, ne)),
            dma((half,)),
            dma((half,)),
            dma((half,)),
            dma((half,)),
            dma((steps, ne)),
            dma((steps, ne)),
            dma((half,)),
            dma((half,)),
        ],
        name="moe_layer",
        cost_estimate=pl.CostEstimate(
            flops=12 * rows * width * hidden, bytes_accessed=6 * width * hidden, transcendentals=rows * hidden
        ),
        compiler_params=pltpu.CompilerParams(
            collective_id=0, has_side_effects=True, vmem_limit_bytes=60 * 1024 * 1024
        ),
    )(tokens, cotangent, routes.T, gates.T, w_gate, w_up, w_down)


def solution(mesh):
    return jax.shard_map(
        shards,
        mesh=mesh,
        in_specs=(
            P(("dp", "expert"), "tensor"),
            P(("dp", "expert"), "tensor"),
            P(("dp", "expert"), None),
            P(("dp", "expert"), None),
            P("expert", None, "tensor"),
            P("expert", None, "tensor"),
            P("expert", "tensor", None),
        ),
        out_specs=(P(("dp", "expert"), "tensor"), P(("dp", "expert"), "tensor")),
        check_vma=False,
    )
```

```python
import functools

import jax
import jax.numpy as jnp
from jax import lax
from jax.experimental import pallas as pl
from jax.experimental.pallas import tpu as pltpu
from jax.sharding import PartitionSpec as P

MESH = pl.DeviceIdType.MESH
F32 = jnp.float32
BF16 = jnp.bfloat16
NT = (((1,), (1,)), ((), ()))


def kernel(
    cap,
    nz,
    tok_hbm,
    cot_hbm,
    routes_hbm,
    gates_hbm,
    wg_hbm,
    wu_hbm,
    wd_hbm,
    mixed_ref,
    grad_ref,
    wg,
    wu,
    wd,
    raw,
    stage,
    slots,
    odd,
    acc,
    hid,
    gg,
    gu,
    qt_ref,
    gs_ref,
    pick_ref,
    routes_ref,
    gates_ref,
    gate_cols,
    odd_out,
    odd_in,
    back,
    home,
    fill_out,
    fill_in,
    far_in,
    chain_out,
    chain_in,
    w_sem,
    raw_s,
    raw_r,
    y_s,
    y_r,
    odd_s,
    odd_r,
    po_s,
    po_r,
    b_s,
    b_r,
    f_s,
    f_r,
    c_s,
    c_r,
):
    dp, me, z = lax.axis_index("dp"), lax.axis_index("expert"), lax.axis_index("tensor")
    ne = lax.axis_size("expert")
    toks, cols = tok_hbm.shape
    hidden = wd.shape[0]
    pair = 2 * cap
    rows = ne * pair
    hop = 3
    last = (nz // 2 - 1) // hop

    def at_z(offset):
        return (dp, me, lax.rem(z + offset + nz, nz))

    def peer(i):
        return (dp, lax.rem(me + i, ne), z)

    def remote(src, dst, send, recv, device):
        return pltpu.make_async_remote_copy(
            src_ref=src, dst_ref=dst, send_sem=send, recv_sem=recv, device_id=device, device_id_type=MESH
        )

    def feat(offset):
        return pl.ds(pl.multiple_of(lax.rem(z + offset + nz, nz) * cols, cols), cols)

    def places(j):
        return {0: (0, 1), 1: (0, 2), last + 1: (1, 3)}.get(j, (0, 4))

    def offset(j, s):
        if j == last + 1 and s == 1:
            return nz // 2
        return (1 if s % 2 else -1) * (hop * j if s < 2 else hop * j - 4)

    def joined(blocks, axis):
        return blocks[0] if len(blocks) == 1 else jnp.concatenate(blocks, axis=axis)

    loads = [
        pltpu.make_async_copy(src, dst, w_sem.at[i])
        for i, (src, dst) in enumerate(((wg_hbm.at[0], wg), (wu_hbm.at[0], wu), (wd_hbm.at[0], wd)))
    ]
    barrier = pltpu.get_barrier_semaphore()
    greeted = [at_z(1), at_z(-1), at_z(hop), at_z(-hop)] + [peer(i) for i in range(1, ne)]
    for device in greeted:
        pl.semaphore_signal(barrier, inc=1, device_id=device, device_id_type=MESH)
    small = [
        pltpu.make_async_copy(src, dst, w_sem.at[3 + i])
        for i, (src, dst) in enumerate(
            (
                (routes_hbm, routes_ref),
                (gates_hbm, gates_ref),
                (tok_hbm, raw.at[0, 0, pl.ds(0, toks)]),
                (cot_hbm, raw.at[0, 0, pl.ds(toks, toks)]),
            )
        )
    ]
    for load in small + loads:
        load.start()
    for load in small:
        load.wait()
    pl.semaphore_wait(barrier, len(greeted))

    def raw_copy(j, d):
        i = 2 * (j - 1) + d
        src = raw.at[0, 0] if j == 1 else raw.at[j - 1, d]
        return remote(src, raw.at[j, d], raw_s.at[i], raw_r.at[i], at_z(hop - 2 * hop * d))

    def fill_copy(j, d):
        i = 2 * last + 2 * (j - 1) + d
        return remote(raw.at[j, d], raw.at[j + 1, 2 + d], raw_s.at[i], raw_r.at[i], at_z(2 * d - 1))

    def far_copy(d):
        i = 4 * last + d
        part = pl.ds(d * toks, toks)
        return remote(raw.at[last, d, part], raw.at[last + 1, 1, part], raw_s.at[i], raw_r.at[i], at_z(1 - 2 * d))

    def exchange(j, out, into, send, recv):
        a, n = places(j)
        for i in range(1, ne):
            to = lax.rem(me + i, ne)
            remote(
                out.at[j, to, pl.ds(a, n)], into.at[j, pl.ds(a, n), me], send.at[j], recv.at[j], peer(i)
            ).start()
        for s in range(a, a + n):
            into[j, s, me] = out[j, me, s]

    def exchanged(j, into, send, recv):
        a, n = places(j)
        every = into.at[j, pl.ds(a, n), pl.ds(0, ne - 1)]
        return remote(every, every, send.at[j], recv.at[j], peer(1))

    def dispatch(j):
        a, n = places(j)
        block = joined([raw[j, s] for s in range(a, a + n)], 1)
        placed = jnp.dot(qt_ref[...], block, preferred_element_type=F32)
        for s in range(n):
            one = (placed[:, s * cols : (s + 1) * cols] * gs_ref[...]).astype(BF16)
            stage[j, :, a + s] = one.reshape(ne, pair, cols)
        exchange(j, stage, slots, y_s, y_r)

    def odd_copy(j, d):
        i = 2 * j + d
        src = slots.at[0, 0] if j == 0 else slots.at[j, d]
        return remote(src, odd.at[j, d], odd_s.at[i], odd_r.at[i], at_z(1 - 2 * d))

    def pass_on(j):
        exchanged(j, slots, y_s, y_r).wait_recv()
        if j < last:
            for d in range(2):
                odd_copy(j, d).start()

    def accumulate(j, o):
        parts = []
        if j is not None:
            a, n = places(j)
            parts += [(slots[j, s], offset(j, s)) for s in range(a, a + n)]
        if o >= 0:
            for d in range(2):
                odd_copy(o, d).wait_recv()
                parts.append((odd[o, d], (2 * d - 1) * (hop * o + 1)))
        lhs = joined([block.reshape(rows, cols) for block, _ in parts], 1)
        for n, w in enumerate((wg, wu, wd)):
            if n < 2:
                rhs = joined([w[feat(x), :] for _, x in parts], 0)
                term = jnp.dot(lhs, rhs, preferred_element_type=F32)
            else:
                rhs = joined([w[:, feat(x)] for _, x in parts], 1)
                term = lax.dot_general(lhs, rhs, NT, preferred_element_type=F32)
            span = slice(n * hidden, (n + 1) * hidden)
            if j == 0:
                acc[:, span] = term
            else:
                acc[:, span] += term

    for d in range(2):
        raw_copy(1, d).start()

    square = lax.broadcasted_iota(jnp.int32, (toks, toks), 0) == lax.broadcasted_iota(
        jnp.int32, (toks, toks), 1
    )

    def column_of(ref, k):
        return jnp.sum(jnp.where(square, ref[k : k + 1, :].astype(F32), 0.0), axis=1, keepdims=True)

    gate_col = [column_of(gates_ref, k) for k in range(2)]
    route_col = [column_of(routes_ref, k) for k in range(2)]
    for k in range(2):
        gate_cols[k] = jnp.broadcast_to(gate_col[k], (toks, cols))
    lane = lax.broadcasted_iota(jnp.int32, (toks, 128), 1)
    chosen = [(route_col[k] == lane.astype(F32)).astype(F32) for k in range(2)]
    before = (
        lax.broadcasted_iota(jnp.int32, (toks, toks), 1) < lax.broadcasted_iota(jnp.int32, (toks, toks), 0)
    ).astype(BF16)
    counts = jnp.dot(before, (chosen[0] + chosen[1]).astype(BF16), preferred_element_type=F32)
    target = [
        jnp.sum(chosen[k] * (counts + (lane * pair).astype(F32)), axis=1, keepdims=True) for k in range(2)
    ]
    wide = lax.broadcasted_iota(jnp.int32, (toks, rows), 1).astype(F32)
    for k in range(2):
        pick_ref[k * toks : (k + 1) * toks, :] = (wide == target[k]).astype(BF16)
    pick_ref[2 * toks : 3 * toks, :] = (
        (wide == target[0] + cap).astype(F32) + (wide == target[1] + cap).astype(F32)
    ).astype(BF16)
    token = lax.broadcasted_iota(jnp.int32, (toks, 2 * toks), 0)
    column = lax.broadcasted_iota(jnp.int32, (toks, 2 * toks), 1)
    diagonal = (column == token) | (column == token + toks)
    down_rows = lax.broadcasted_iota(jnp.int32, (rows, 2 * toks), 0).astype(F32)
    lanes1 = lax.broadcasted_iota(jnp.int32, (1, 2 * toks), 1)
    second = jnp.where(lanes1 < toks, 0.0, float(cap))
    placing, scale = 0.0, 0.0
    for k in range(2):
        row_target = jnp.sum(jnp.where(diagonal, target[k], 0.0), axis=0, keepdims=True) + second
        row_gate = jnp.sum(jnp.where(diagonal, gate_col[k], 0.0), axis=0, keepdims=True)
        row_gate = jnp.where(lanes1 < toks, 1.0, row_gate)
        hit = down_rows == row_target
        placing = placing + hit.astype(F32)
        scale = scale + jnp.sum(jnp.where(hit, row_gate, 0.0), axis=1, keepdims=True)
    qt_ref[...] = placing.astype(BF16)
    gs_ref[...] = jnp.broadcast_to(scale, (rows, 128))

    dispatch(0)
    for j in range(1, last + 1):
        for d in range(2):
            raw_copy(j, d).wait_recv()
            if j < last:
                raw_copy(j + 1, d).start()
            else:
                far_copy(d).start()
            fill_copy(j, d).start()
        if j > 1:
            for d in range(2):
                fill_copy(j - 1, d).wait_recv()
        dispatch(j)
        pass_on(j - 1)
        if j == 1:
            for load in loads:
                load.wait()
        accumulate(j - 1, j - 3)
        for d in range(2):
            raw_copy(j, d).wait_send()
    for d in range(2):
        fill_copy(last, d).wait_recv()
        far_copy(d).wait_recv()
    dispatch(last + 1)
    pass_on(last)
    accumulate(last, last - 2)
    pass_on(last + 1)
    accumulate(last + 1, last - 1)

    for j in range(ne // 2):
        top = 2 * pair * j
        mine = jnp.concatenate([acc[top : top + cap, :], acc[top + pair : top + pair + cap, :]], axis=0)
        gh = jnp.concatenate(
            [acc[top + cap : top + pair, 2 * hidden :], acc[top + pair + cap : top + 2 * pair, 2 * hidden :]],
            axis=0,
        )
        gate, up = mine[:, :hidden], mine[:, hidden : 2 * hidden]
        sigmoid = jax.nn.sigmoid(gate)
        active = gate * sigmoid
        span = slice(pair * j, pair * (j + 1))
        hid[span, :] = (active * up).astype(BF16)
        gg[span, :] = (gh * up * sigmoid * (1.0 + gate * (1.0 - sigmoid))).astype(BF16)
        gu[span, :] = (gh * active).astype(BF16)

    def partial(offsets):
        down = joined([wd[:, feat(o)] for o in offsets], 1)
        gate = joined([wg[feat(o), :] for o in offsets], 0)
        up = joined([wu[feat(o), :] for o in offsets], 0)
        out = jnp.dot(hid[...], down, preferred_element_type=F32)
        grad = lax.dot_general(gg[...], gate, NT, preferred_element_type=F32)
        grad = grad + lax.dot_general(gu[...], up, NT, preferred_element_type=F32)
        parts = []
        for e in range(ne):
            parts += [out[cap * e : cap * (e + 1)], grad[cap * e : cap * (e + 1)]]
        both = jnp.concatenate(parts, axis=0)
        return [both[:, s * cols : (s + 1) * cols] for s in range(len(offsets))]

    def po_copy(j, d):
        i = 2 * j + d
        return remote(odd_out.at[j, d], odd_in.at[j, d], po_s.at[i], po_r.at[i], at_z(2 * d - 1))

    def send_odd(j):
        for d, block in enumerate(partial([-hop * j - 1, hop * j + 1])):
            odd_out[j, d] = block.astype(BF16)
            po_copy(j, d).start()

    def send_group(j):
        a, n = places(j)
        total = partial([offset(j, s) for s in range(a, a + n)])
        if j < last:
            for d in range(2):
                po_copy(j, d).wait_recv()
                to = 0 if j == 0 else d
                total[to] = total[to] + odd_in[j, d].astype(F32)
        for s in range(n):
            back[j, :, a + s] = total[s].astype(BF16).reshape(ne, pair, cols)
        exchange(j, back, home, b_s, b_r)

    def back_fill(j, d):
        i = 2 * (j - 1) + d
        return remote(fill_out.at[j, d], fill_in.at[j, d], f_s.at[i], f_r.at[i], at_z(1 - 2 * d))

    def back_far(d):
        i = 2 * last + d
        part = pl.ds(d * toks, toks)
        return remote(fill_out.at[0, 0, part], far_in.at[part], f_s.at[i], f_r.at[i], at_z(2 * d - 1))

    def chain_copy(j, d):
        i = 2 * (j - 1) + d
        return remote(chain_out.at[j, d], chain_in.at[j - 1, d], c_s.at[i], c_r.at[i], at_z(2 * hop * d - hop))

    def combine(j):
        a, n = places(j)
        exchanged(j, home, b_s, b_r).wait_recv()
        block = joined([home[j, s].reshape(rows, cols) for s in range(a, a + n)], 1)
        picked = jnp.dot(pick_ref[...], block, preferred_element_type=F32)
        sums = [None] * 4
        for s in range(n):
            one = picked[:, s * cols : (s + 1) * cols]
            mixed = gate_cols[0] * one[:toks] + gate_cols[1] * one[toks : 2 * toks]
            sums[a + s] = jnp.concatenate([mixed, one[2 * toks :]], axis=0)
        if j > 1:
            for d in range(2):
                fill_out[j - 1, d] = sums[2 + d].astype(BF16)
                back_fill(j - 1, d).start()
        if j == last + 1:
            fill_out[0, 0] = sums[1].astype(BF16)
            for d in range(2):
                back_far(d).start()
        return sums

    def chain_step(j):
        sums = combine(j)
        for d in range(2):
            back_fill(j, d).wait_recv()
            total = sums[d] + fill_in[j, d].astype(F32)
            if j == last:
                back_far(d).wait_recv()
                half = far_in[d * toks : (d + 1) * toks, :].astype(F32)
                none = jnp.zeros_like(half)
                total = total + jnp.concatenate([half, none] if d == 0 else [none, half], axis=0)
            else:
                chain_copy(j + 1, d).wait_recv()
                total = total + chain_in[j, d].astype(F32)
            chain_out[j, d] = total.astype(BF16)
            chain_copy(j, d).start()

    send_group(last + 1)
    send_odd(last - 1)
    send_group(last)
    send_odd(last - 2)
    combine(last + 1)
    send_group(last - 1)
    send_odd(last - 3)
    chain_step(last)
    for j in range(last - 2, 0, -1):
        send_group(j)
        if j > 1:
            send_odd(j - 2)
        chain_step(j + 1)
    send_group(0)
    chain_step(1)
    sums = combine(0)[0]
    for d in range(2):
        for j in range(1, last + 1):
            fill_copy(j, d).wait_send()
            back_fill(j, d).wait_send()
            chain_copy(j, d).wait_send()
        far_copy(d).wait_send()
        back_far(d).wait_send()
        for j in range(last):
            odd_copy(j, d).wait_send()
            po_copy(j, d).wait_send()
    for j in range(last + 2):
        exchanged(j, slots, y_s, y_r).wait_send()
        exchanged(j, home, b_s, b_r).wait_send()
    for d in range(2):
        chain_copy(1, d).wait_recv()
        sums = sums + chain_in[0, d].astype(F32)
    mixed_ref[...] = sums[:toks].astype(BF16)
    grad_ref[...] = sums[toks:].astype(BF16)


def shards(tokens, cotangent, routes, gates, w_gate, w_up, w_down):
    ne, nz = lax.axis_size("expert"), lax.axis_size("tensor")
    toks, cols = tokens.shape
    width, hidden = w_gate.shape[1:]
    cap = toks * routes.shape[1] * 3 // (2 * ne)
    pair = 2 * cap
    rows = ne * pair
    last = (nz // 2 - 1) // 3
    groups = last + 2
    vmem = pl.BlockSpec(memory_space=pltpu.VMEM)
    hbm = pl.BlockSpec(memory_space=pl.ANY)
    dma = pltpu.SemaphoreType.DMA
    out = jax.ShapeDtypeStruct((toks, cols), BF16)
    staged = pltpu.VMEM((groups, ne, 4, pair, cols), BF16)
    landed = pltpu.VMEM((groups, 4, ne, pair, cols), BF16)
    flat = pltpu.VMEM((last, 2, rows, cols), BF16)
    tokens_of = pltpu.VMEM((last + 1, 2, 2 * toks, cols), BF16)
    return pl.pallas_call(
        functools.partial(kernel, cap, nz),
        out_shape=(out, out),
        in_specs=[hbm] * 7,
        out_specs=(vmem, vmem),
        scratch_shapes=[
            pltpu.VMEM((width, hidden), BF16),
            pltpu.VMEM((width, hidden), BF16),
            pltpu.VMEM((hidden, width), BF16),
            pltpu.VMEM((groups, 4, 2 * toks, cols), BF16),
            staged,
            landed,
            pltpu.VMEM((last, 2, ne, pair, cols), BF16),
            pltpu.VMEM((rows, 3 * hidden), F32),
            pltpu.VMEM((rows // 2, hidden), BF16),
            pltpu.VMEM((rows // 2, hidden), BF16),
            pltpu.VMEM((rows // 2, hidden), BF16),
            pltpu.VMEM((rows, 2 * toks), BF16),
            pltpu.VMEM((rows, 128), F32),
            pltpu.VMEM((3 * toks, rows), BF16),
            pltpu.VMEM((2, toks), jnp.int32),
            pltpu.VMEM((2, toks), F32),
            pltpu.VMEM((2, toks, cols), F32),
            flat,
            flat,
            staged,
            landed,
            tokens_of,
            tokens_of,
            pltpu.VMEM((2 * toks, cols), BF16),
            tokens_of,
            tokens_of,
            dma((7,)),
            dma((4 * last + 2,)),
            dma((4 * last + 2,)),
            dma((groups,)),
            dma((groups,)),
            dma((2 * last,)),
            dma((2 * last,)),
            dma((2 * last,)),
            dma((2 * last,)),
            dma((groups,)),
            dma((groups,)),
            dma((2 * last + 2,)),
            dma((2 * last + 2,)),
            dma((2 * last,)),
            dma((2 * last,)),
        ],
        name="moe_layer",
        cost_estimate=pl.CostEstimate(
            flops=12 * rows * width * hidden, bytes_accessed=6 * width * hidden, transcendentals=rows * hidden
        ),
        compiler_params=pltpu.CompilerParams(
            collective_id=0, has_side_effects=True, vmem_limit_bytes=60 * 1024 * 1024
        ),
    )(tokens, cotangent, routes.T, gates.T, w_gate, w_up, w_down)


def solution(mesh):
    return jax.shard_map(
        shards,
        mesh=mesh,
        in_specs=(
            P(("dp", "expert"), "tensor"),
            P(("dp", "expert"), "tensor"),
            P(("dp", "expert"), None),
            P(("dp", "expert"), None),
            P("expert", None, "tensor"),
            P("expert", None, "tensor"),
            P("expert", "tensor", None),
        ),
        out_specs=(P(("dp", "expert"), "tensor"), P(("dp", "expert"), "tensor")),
        check_vma=False,
    )
```

```python
import functools

import jax
import jax.numpy as jnp
from jax import lax
from jax.experimental import pallas as pl
from jax.experimental.pallas import tpu as pltpu
from jax.sharding import PartitionSpec as P

MESH = pl.DeviceIdType.MESH
F32 = jnp.float32
BF16 = jnp.bfloat16
NT = (((1,), (1,)), ((), ()))


def kernel(
    cap,
    nz,
    tok_hbm,
    cot_hbm,
    routes_hbm,
    gates_hbm,
    wg_hbm,
    wu_hbm,
    wd_hbm,
    out_ref,
    wg,
    wu,
    wd,
    raw,
    stage,
    slots,
    odd,
    acc,
    hid,
    gg,
    gu,
    qt_ref,
    gs_ref,
    pick_ref,
    routes_ref,
    gates_ref,
    gate_cols,
    odd_out,
    odd_in,
    back,
    home,
    fill_out,
    fill_in,
    far_in,
    chain_out,
    chain_in,
    w_sem,
    raw_s,
    raw_r,
    y_s,
    y_r,
    odd_s,
    odd_r,
    po_s,
    po_r,
    b_s,
    b_r,
    f_s,
    f_r,
    c_s,
    c_r,
):
    dp, me, z = lax.axis_index("dp"), lax.axis_index("expert"), lax.axis_index("tensor")
    ne = lax.axis_size("expert")
    toks, cols = tok_hbm.shape
    hidden = wd.shape[0]
    pair = 2 * cap
    rows = ne * pair
    hop = 3
    last = (nz // 2 - 1) // hop

    def at_z(offset):
        return (dp, me, lax.rem(z + offset + nz, nz))

    def peer(i):
        return (dp, lax.rem(me + i, ne), z)

    def remote(src, dst, send, recv, device):
        return pltpu.make_async_remote_copy(
            src_ref=src, dst_ref=dst, send_sem=send, recv_sem=recv, device_id=device, device_id_type=MESH
        )

    def feat(offset):
        return pl.ds(pl.multiple_of(lax.rem(z + offset + nz, nz) * cols, cols), cols)

    def places(j):
        return {0: (0, 1), last: (0, 2), last + 1: (1, 3)}.get(j, (0, 4))

    def offset(j, s):
        if j == last + 1 and s == 1:
            return nz // 2
        return (1 if s % 2 else -1) * (hop * j if s < 2 else hop * min(j, last) - 1)

    def joined(blocks, axis):
        return blocks[0] if len(blocks) == 1 else jnp.concatenate(blocks, axis=axis)

    loads = [
        pltpu.make_async_copy(src, dst, w_sem.at[i])
        for i, (src, dst) in enumerate(((wg_hbm.at[0], wg), (wu_hbm.at[0], wu), (wd_hbm.at[0], wd)))
    ]
    barrier = pltpu.get_barrier_semaphore()
    greeted = [at_z(sign * n) for n in (1, 2, hop, 4) for sign in (1, -1)] + [peer(i) for i in range(1, ne)]
    for device in greeted:
        pl.semaphore_signal(barrier, inc=1, device_id=device, device_id_type=MESH)
    small = [
        pltpu.make_async_copy(src, dst, w_sem.at[3 + i])
        for i, (src, dst) in enumerate(
            (
                (routes_hbm, routes_ref),
                (gates_hbm, gates_ref),
                (tok_hbm, raw.at[0, 0, pl.ds(0, toks)]),
                (cot_hbm, raw.at[0, 0, pl.ds(toks, toks)]),
            )
        )
    ]
    for load in small + loads:
        load.start()
    for load in small:
        load.wait()
    pl.semaphore_wait(barrier, len(greeted))

    def raw_copy(j, d):
        i = 2 * (j - 1) + d
        src = raw.at[0, 0] if j == 1 else raw.at[j - 1, d]
        return remote(src, raw.at[j, d], raw_s.at[i], raw_r.at[i], at_z(hop - 2 * hop * d))

    def filled(j):
        return j + 1 if j < last - 1 else last + 1

    def fill_copy(j, d):
        i = 2 * last + 2 * j + d
        src = raw.at[0, 0] if j == 0 else raw.at[j, d]
        return remote(src, raw.at[filled(j), 2 + d], raw_s.at[i], raw_r.at[i], at_z(2 - 4 * d))

    def far_copy(d):
        i = 4 * last + d
        part = pl.ds(d * toks, toks)
        return remote(
            raw.at[last - 1, d, part], raw.at[last + 1, 1, part], raw_s.at[i], raw_r.at[i], at_z(4 - 8 * d)
        )

    def exchange(j, out, into, send, recv):
        a, n = places(j)
        for i in range(1, ne):
            to = lax.rem(me + i, ne)
            remote(
                out.at[j, to, pl.ds(a, n)], into.at[j, pl.ds(a, n), me], send.at[j], recv.at[j], peer(i)
            ).start()
        for s in range(a, a + n):
            into[j, s, me] = out[j, me, s]

    def exchanged(j, into, send, recv):
        a, n = places(j)
        every = into.at[j, pl.ds(a, n), pl.ds(0, ne - 1)]
        return remote(every, every, send.at[j], recv.at[j], peer(1))

    def dispatch(j):
        a, n = places(j)
        block = joined([raw[j, s] for s in range(a, a + n)], 1)
        placed = jnp.dot(qt_ref[...], block, preferred_element_type=F32)
        for s in range(n):
            one = (placed[:, s * cols : (s + 1) * cols] * gs_ref[...]).astype(BF16)
            stage[j, :, a + s] = one.reshape(ne, pair, cols)
        exchange(j, stage, slots, y_s, y_r)

    def odd_copy(j, d):
        i = 2 * j + d
        src = slots.at[0, 0] if j == 0 else slots.at[j, d]
        return remote(src, odd.at[j, d], odd_s.at[i], odd_r.at[i], at_z(1 - 2 * d))

    def pass_on(j):
        exchanged(j, slots, y_s, y_r).wait_recv()
        if j < last:
            for d in range(2):
                odd_copy(j, d).start()

    def accumulate(j, o):
        parts = []
        if j is not None:
            a, n = places(j)
            parts += [(slots[j, s], offset(j, s)) for s in range(a, a + n)]
        if o >= 0:
            for d in range(2):
                odd_copy(o, d).wait_recv()
                parts.append((odd[o, d], (2 * d - 1) * (hop * o + 1)))
        lhs = joined([block.reshape(rows, cols) for block, _ in parts], 1)
        for n, w in enumerate((wg, wu, wd)):
            if n < 2:
                rhs = joined([w[feat(x), :] for _, x in parts], 0)
                term = jnp.dot(lhs, rhs, preferred_element_type=F32)
            else:
                rhs = joined([w[:, feat(x)] for _, x in parts], 1)
                term = lax.dot_general(lhs, rhs, NT, preferred_element_type=F32)
            span = slice(n * hidden, (n + 1) * hidden)
            if j == 0:
                acc[:, span] = term
            else:
                acc[:, span] += term

    for d in range(2):
        raw_copy(1, d).start()
        fill_copy(0, d).start()

    square = lax.broadcasted_iota(jnp.int32, (toks, toks), 0) == lax.broadcasted_iota(
        jnp.int32, (toks, toks), 1
    )

    def column_of(ref, k):
        return jnp.sum(jnp.where(square, ref[k : k + 1, :].astype(F32), 0.0), axis=1, keepdims=True)

    gate_col = [column_of(gates_ref, k) for k in range(2)]
    route_col = [column_of(routes_ref, k) for k in range(2)]
    for k in range(2):
        gate_cols[k] = jnp.broadcast_to(gate_col[k], (toks, cols))
    lane = lax.broadcasted_iota(jnp.int32, (toks, 128), 1)
    chosen = [(route_col[k] == lane.astype(F32)).astype(F32) for k in range(2)]
    before = (
        lax.broadcasted_iota(jnp.int32, (toks, toks), 1) < lax.broadcasted_iota(jnp.int32, (toks, toks), 0)
    ).astype(BF16)
    counts = jnp.dot(before, (chosen[0] + chosen[1]).astype(BF16), preferred_element_type=F32)
    target = [
        jnp.sum(chosen[k] * (counts + (lane * pair).astype(F32)), axis=1, keepdims=True) for k in range(2)
    ]
    wide = lax.broadcasted_iota(jnp.int32, (toks, rows), 1).astype(F32)
    for k in range(2):
        pick_ref[k * toks : (k + 1) * toks, :] = (wide == target[k]).astype(BF16)
    pick_ref[2 * toks : 3 * toks, :] = (
        (wide == target[0] + cap).astype(F32) + (wide == target[1] + cap).astype(F32)
    ).astype(BF16)
    token = lax.broadcasted_iota(jnp.int32, (toks, 2 * toks), 0)
    column = lax.broadcasted_iota(jnp.int32, (toks, 2 * toks), 1)
    diagonal = (column == token) | (column == token + toks)
    down_rows = lax.broadcasted_iota(jnp.int32, (rows, 2 * toks), 0).astype(F32)
    lanes1 = lax.broadcasted_iota(jnp.int32, (1, 2 * toks), 1)
    second = jnp.where(lanes1 < toks, 0.0, float(cap))
    placing, scale = 0.0, 0.0
    for k in range(2):
        row_target = jnp.sum(jnp.where(diagonal, target[k], 0.0), axis=0, keepdims=True) + second
        row_gate = jnp.sum(jnp.where(diagonal, gate_col[k], 0.0), axis=0, keepdims=True)
        row_gate = jnp.where(lanes1 < toks, 1.0, row_gate)
        hit = down_rows == row_target
        placing = placing + hit.astype(F32)
        scale = scale + jnp.sum(jnp.where(hit, row_gate, 0.0), axis=1, keepdims=True)
    qt_ref[...] = placing.astype(BF16)
    gs_ref[...] = jnp.broadcast_to(scale, (rows, 128))

    dispatch(0)
    for j in range(1, last):
        for d in range(2):
            raw_copy(j, d).wait_recv()
            raw_copy(j + 1, d).start()
            fill_copy(j, d).start()
            if j == last - 1:
                far_copy(d).start()
        for d in range(2):
            fill_copy(j - 1, d).wait_recv()
        dispatch(j)
        pass_on(j - 1)
        if j == 1:
            for load in loads:
                load.wait()
        accumulate(j - 1, j - 3)
        for d in range(2):
            raw_copy(j, d).wait_send()
    for d in range(2):
        raw_copy(last, d).wait_recv()
    dispatch(last)
    for d in range(2):
        fill_copy(last - 1, d).wait_recv()
        far_copy(d).wait_recv()
    dispatch(last + 1)
    pass_on(last - 1)
    accumulate(last - 1, last - 3)
    pass_on(last)
    accumulate(last, last - 2)
    pass_on(last + 1)
    accumulate(last + 1, last - 1)

    for j in range(ne // 2):
        top = 2 * pair * j
        mine = jnp.concatenate([acc[top : top + cap, :], acc[top + pair : top + pair + cap, :]], axis=0)
        gh = jnp.concatenate(
            [acc[top + cap : top + pair, 2 * hidden :], acc[top + pair + cap : top + 2 * pair, 2 * hidden :]],
            axis=0,
        )
        gate, up = mine[:, :hidden], mine[:, hidden : 2 * hidden]
        sigmoid = jax.nn.sigmoid(gate)
        active = gate * sigmoid
        span = slice(pair * j, pair * (j + 1))
        hid[span, :] = (active * up).astype(BF16)
        gg[span, :] = (gh * up * sigmoid * (1.0 + gate * (1.0 - sigmoid))).astype(BF16)
        gu[span, :] = (gh * active).astype(BF16)

    def partial(offsets):
        down = joined([wd[:, feat(o)] for o in offsets], 1)
        gate = joined([wg[feat(o), :] for o in offsets], 0)
        up = joined([wu[feat(o), :] for o in offsets], 0)
        out = jnp.dot(hid[...], down, preferred_element_type=F32)
        grad = lax.dot_general(gg[...], gate, NT, preferred_element_type=F32)
        grad = grad + lax.dot_general(gu[...], up, NT, preferred_element_type=F32)
        parts = []
        for e in range(ne):
            parts += [out[cap * e : cap * (e + 1)], grad[cap * e : cap * (e + 1)]]
        both = jnp.concatenate(parts, axis=0)
        return [both[:, s * cols : (s + 1) * cols] for s in range(len(offsets))]

    def po_copy(j, d):
        i = 2 * j + d
        return remote(odd_out.at[j, d], odd_in.at[j, d], po_s.at[i], po_r.at[i], at_z(2 * d - 1))

    def send_odd(j):
        for d, block in enumerate(partial([-hop * j - 1, hop * j + 1])):
            odd_out[j, d] = block.astype(BF16)
            po_copy(j, d).start()

    def send_group(j):
        a, n = places(j)
        total = partial([offset(j, s) for s in range(a, a + n)])
        if j < last:
            for d in range(2):
                po_copy(j, d).wait_recv()
                to = 0 if j == 0 else d
                total[to] = total[to] + odd_in[j, d].astype(F32)
        for s in range(n):
            back[j, :, a + s] = total[s].astype(BF16).reshape(ne, pair, cols)
        exchange(j, back, home, b_s, b_r)

    def back_fill(j, d):
        i = 2 * j + d
        return remote(fill_out.at[j, d], fill_in.at[j, d], f_s.at[i], f_r.at[i], at_z(4 * d - 2))

    def back_far(d):
        i = 2 * last + d
        part = pl.ds(d * toks, toks)
        return remote(fill_out.at[last, 0, part], far_in.at[part], f_s.at[i], f_r.at[i], at_z(8 * d - 4))

    def chain_copy(j, d):
        i = 2 * (j - 1) + d
        return remote(chain_out.at[j, d], chain_in.at[j - 1, d], c_s.at[i], c_r.at[i], at_z(2 * hop * d - hop))

    def combine(j):
        a, n = places(j)
        exchanged(j, home, b_s, b_r).wait_recv()
        block = joined([home[j, s].reshape(rows, cols) for s in range(a, a + n)], 1)
        picked = jnp.dot(pick_ref[...], block, preferred_element_type=F32)
        sums = [None] * 4
        for s in range(n):
            one = picked[:, s * cols : (s + 1) * cols]
            mixed = gate_cols[0] * one[:toks] + gate_cols[1] * one[toks : 2 * toks]
            sums[a + s] = jnp.concatenate([mixed, one[2 * toks :]], axis=0)
        for place in range(last):
            if filled(place) == j:
                for d in range(2):
                    fill_out[place, d] = sums[2 + d].astype(BF16)
                    back_fill(place, d).start()
        if j == last + 1:
            fill_out[last, 0] = sums[1].astype(BF16)
            for d in range(2):
                back_far(d).start()
        return sums

    def chain_step(j):
        sums = combine(j)
        for d in range(2):
            total = sums[d]
            if j < last:
                back_fill(j, d).wait_recv()
                chain_copy(j + 1, d).wait_recv()
                total = total + fill_in[j, d].astype(F32) + chain_in[j, d].astype(F32)
            if j == last - 1:
                back_far(d).wait_recv()
                half = far_in[d * toks : (d + 1) * toks, :].astype(F32)
                none = jnp.zeros_like(half)
                total = total + jnp.concatenate([half, none] if d == 0 else [none, half], axis=0)
            chain_out[j, d] = total.astype(BF16)
            chain_copy(j, d).start()

    send_group(last)
    send_group(last + 1)
    send_odd(last - 1)
    send_odd(last - 2)
    chain_step(last)
    combine(last + 1)
    send_group(last - 1)
    send_odd(last - 3)
    for j in range(last - 2, 0, -1):
        send_group(j)
        if j > 1:
            send_odd(j - 2)
        chain_step(j + 1)
    send_group(0)
    chain_step(1)
    sums = combine(0)[0]
    for d in range(2):
        for j in range(1, last + 1):
            fill_copy(j - 1, d).wait_send()
            back_fill(j - 1, d).wait_send()
            chain_copy(j, d).wait_send()
        raw_copy(last, d).wait_send()
        far_copy(d).wait_send()
        back_far(d).wait_send()
        for j in range(last):
            odd_copy(j, d).wait_send()
            po_copy(j, d).wait_send()
    for j in range(last + 2):
        exchanged(j, slots, y_s, y_r).wait_send()
        exchanged(j, home, b_s, b_r).wait_send()
    for d in range(2):
        back_fill(0, d).wait_recv()
        chain_copy(1, d).wait_recv()
        sums = sums + fill_in[0, d].astype(F32) + chain_in[0, d].astype(F32)
    out_ref[0] = sums[:toks].astype(BF16)
    out_ref[1] = sums[toks:].astype(BF16)


def shards(tokens, cotangent, routes, gates, w_gate, w_up, w_down):
    ne, nz = lax.axis_size("expert"), lax.axis_size("tensor")
    toks, cols = tokens.shape
    width, hidden = w_gate.shape[1:]
    cap = toks * routes.shape[1] * 3 // (2 * ne)
    pair = 2 * cap
    rows = ne * pair
    last = (nz // 2 - 1) // 3
    groups = last + 2
    vmem = pl.BlockSpec(memory_space=pltpu.VMEM)
    hbm = pl.BlockSpec(memory_space=pl.ANY)
    dma = pltpu.SemaphoreType.DMA
    out = jax.ShapeDtypeStruct((2, toks, cols), BF16)
    staged = pltpu.VMEM((groups, ne, 4, pair, cols), BF16)
    landed = pltpu.VMEM((groups, 4, ne, pair, cols), BF16)
    flat = pltpu.VMEM((last, 2, rows, cols), BF16)
    tokens_of = pltpu.VMEM((last + 1, 2, 2 * toks, cols), BF16)
    both = pl.pallas_call(
        functools.partial(kernel, cap, nz),
        out_shape=out,
        in_specs=[hbm] * 7,
        out_specs=vmem,
        scratch_shapes=[
            pltpu.VMEM((width, hidden), BF16),
            pltpu.VMEM((width, hidden), BF16),
            pltpu.VMEM((hidden, width), BF16),
            pltpu.VMEM((groups, 4, 2 * toks, cols), BF16),
            staged,
            landed,
            pltpu.VMEM((last, 2, ne, pair, cols), BF16),
            pltpu.VMEM((rows, 3 * hidden), F32),
            pltpu.VMEM((rows // 2, hidden), BF16),
            pltpu.VMEM((rows // 2, hidden), BF16),
            pltpu.VMEM((rows // 2, hidden), BF16),
            pltpu.VMEM((rows, 2 * toks), BF16),
            pltpu.VMEM((rows, 128), F32),
            pltpu.VMEM((3 * toks, rows), BF16),
            pltpu.VMEM((2, toks), jnp.int32),
            pltpu.VMEM((2, toks), F32),
            pltpu.VMEM((2, toks, cols), F32),
            flat,
            flat,
            staged,
            landed,
            tokens_of,
            tokens_of,
            pltpu.VMEM((2 * toks, cols), BF16),
            tokens_of,
            tokens_of,
            dma((7,)),
            dma((4 * last + 2,)),
            dma((4 * last + 2,)),
            dma((groups,)),
            dma((groups,)),
            dma((2 * last,)),
            dma((2 * last,)),
            dma((2 * last,)),
            dma((2 * last,)),
            dma((groups,)),
            dma((groups,)),
            dma((2 * last + 2,)),
            dma((2 * last + 2,)),
            dma((2 * last,)),
            dma((2 * last,)),
        ],
        name="moe_layer",
        cost_estimate=pl.CostEstimate(
            flops=12 * rows * width * hidden, bytes_accessed=6 * width * hidden, transcendentals=rows * hidden
        ),
        compiler_params=pltpu.CompilerParams(
            collective_id=0, has_side_effects=True, vmem_limit_bytes=60 * 1024 * 1024
        ),
    )(tokens, cotangent, routes.T, gates.T, w_gate, w_up, w_down)
    return both[0], both[1]


def solution(mesh):
    return jax.shard_map(
        shards,
        mesh=mesh,
        in_specs=(
            P(("dp", "expert"), "tensor"),
            P(("dp", "expert"), "tensor"),
            P(("dp", "expert"), None),
            P(("dp", "expert"), None),
            P("expert", None, "tensor"),
            P("expert", None, "tensor"),
            P("expert", "tensor", None),
        ),
        out_specs=(P(("dp", "expert"), "tensor"), P(("dp", "expert"), "tensor")),
        check_vma=False,
    )
```

```python
import functools

import jax
import jax.numpy as jnp
from jax import lax
from jax.experimental import pallas as pl
from jax.experimental.pallas import tpu as pltpu
from jax.sharding import PartitionSpec as P

MESH = pl.DeviceIdType.MESH
F32 = jnp.float32
BF16 = jnp.bfloat16
NT = (((1,), (1,)), ((), ()))
OUTER = (4,)


def kernel(
    cap,
    nz,
    tok_hbm,
    cot_hbm,
    routes_hbm,
    gates_hbm,
    wg_hbm,
    wu_hbm,
    wd_hbm,
    out_ref,
    wg,
    wu,
    wd,
    raw,
    stage,
    slots,
    odd,
    acc,
    hid,
    gg,
    gu,
    qt_ref,
    gs_ref,
    pick_ref,
    routes_ref,
    gates_ref,
    gate_cols,
    odd_out,
    odd_in,
    back,
    home,
    fill_out,
    fill_in,
    far_in,
    chain_out,
    chain_in,
    w_sem,
    raw_s,
    raw_r,
    y_s,
    y_r,
    odd_s,
    odd_r,
    po_s,
    po_r,
    b_s,
    b_r,
    f_s,
    f_r,
    c_s,
    c_r,
):
    dp, me, z = lax.axis_index("dp"), lax.axis_index("expert"), lax.axis_index("tensor")
    ne = lax.axis_size("expert")
    toks, cols = tok_hbm.shape
    hidden = wd.shape[0]
    pair = 2 * cap
    rows = ne * pair
    hop = 3
    last = (nz // 2 - 1) // hop

    def at_z(offset):
        return (dp, me, lax.rem(z + offset + nz, nz))

    def peer(i):
        return (dp, lax.rem(me + i, ne), z)

    def remote(src, dst, send, recv, device):
        return pltpu.make_async_remote_copy(
            src_ref=src, dst_ref=dst, send_sem=send, recv_sem=recv, device_id=device, device_id_type=MESH
        )

    def feat(offset):
        return pl.ds(pl.multiple_of(lax.rem(z + offset + nz, nz) * cols, cols), cols)

    def places(j):
        return {0: (0, 1), 1: (0, 2), last + 1: (1, 3)}.get(j, (0, 6 if j - 1 in OUTER else 4))

    def offset(j, s):
        if j == last + 1 and s == 1:
            return nz // 2
        return (1 if s % 2 else -1) * (hop * j - (0, 4, 2)[s // 2])

    def joined(blocks, axis):
        return blocks[0] if len(blocks) == 1 else jnp.concatenate(blocks, axis=axis)

    loads = [
        pltpu.make_async_copy(src, dst, w_sem.at[i])
        for i, (src, dst) in enumerate(((wg_hbm.at[0], wg), (wu_hbm.at[0], wu), (wd_hbm.at[0], wd)))
    ]
    barrier = pltpu.get_barrier_semaphore()
    greeted = [at_z(1), at_z(-1), at_z(hop), at_z(-hop)] + [peer(i) for i in range(1, ne)]
    for device in greeted:
        pl.semaphore_signal(barrier, inc=1, device_id=device, device_id_type=MESH)
    small = [
        pltpu.make_async_copy(src, dst, w_sem.at[3 + i])
        for i, (src, dst) in enumerate(
            (
                (routes_hbm, routes_ref),
                (gates_hbm, gates_ref),
                (tok_hbm, raw.at[0, 0, pl.ds(0, toks)]),
                (cot_hbm, raw.at[0, 0, pl.ds(toks, toks)]),
            )
        )
    ]
    for load in small + loads:
        load.start()
    for load in small:
        load.wait()
    pl.semaphore_wait(barrier, len(greeted))

    def raw_copy(j, d):
        i = 2 * (j - 1) + d
        src = raw.at[0, 0] if j == 1 else raw.at[j - 1, d]
        return remote(src, raw.at[j, d], raw_s.at[i], raw_r.at[i], at_z(hop - 2 * hop * d))

    def fill_copy(j, d):
        i = 2 * last + 2 * (j - 1) + d
        return remote(raw.at[j, d], raw.at[j + 1, 2 + d], raw_s.at[i], raw_r.at[i], at_z(2 * d - 1))

    def far_copy(d):
        i = 4 * last + d
        part = pl.ds(d * toks, toks)
        return remote(raw.at[last, d, part], raw.at[last + 1, 1, part], raw_s.at[i], raw_r.at[i], at_z(1 - 2 * d))

    def outer_copy(j, d):
        i = 4 * last + 2 + 2 * j + d
        return remote(raw.at[j, d], raw.at[j + 1, 4 + d], raw_s.at[i], raw_r.at[i], at_z(1 - 2 * d))

    def exchange(j, out, into, send, recv):
        a, n = places(j)
        for i in range(1, ne):
            to = lax.rem(me + i, ne)
            remote(
                out.at[j, to, pl.ds(a, n)], into.at[j, pl.ds(a, n), me], send.at[j], recv.at[j], peer(i)
            ).start()
        for s in range(a, a + n):
            into[j, s, me] = out[j, me, s]

    def exchanged(j, into, send, recv):
        a, n = places(j)
        every = into.at[j, pl.ds(a, n), pl.ds(0, ne - 1)]
        return remote(every, every, send.at[j], recv.at[j], peer(1))

    def dispatch(j):
        a, n = places(j)
        block = joined([raw[j, s] for s in range(a, a + n)], 1)
        placed = jnp.dot(qt_ref[...], block, preferred_element_type=F32)
        for s in range(n):
            one = (placed[:, s * cols : (s + 1) * cols] * gs_ref[...]).astype(BF16)
            stage[j, :, a + s] = one.reshape(ne, pair, cols)
        exchange(j, stage, slots, y_s, y_r)

    def odd_copy(j, d):
        i = 2 * j + d
        src = slots.at[0, 0] if j == 0 else slots.at[j, d]
        return remote(src, odd.at[j, d], odd_s.at[i], odd_r.at[i], at_z(1 - 2 * d))

    def pass_on(j):
        exchanged(j, slots, y_s, y_r).wait_recv()
        if j < last and j not in OUTER:
            for d in range(2):
                odd_copy(j, d).start()

    def accumulate(j, o):
        parts = []
        if j is not None:
            a, n = places(j)
            parts += [(slots[j, s], offset(j, s)) for s in range(a, a + n)]
        if o >= 0 and o not in OUTER:
            for d in range(2):
                odd_copy(o, d).wait_recv()
                parts.append((odd[o, d], (2 * d - 1) * (hop * o + 1)))
        lhs = joined([block.reshape(rows, cols) for block, _ in parts], 1)
        for n, w in enumerate((wg, wu, wd)):
            if n < 2:
                rhs = joined([w[feat(x), :] for _, x in parts], 0)
                term = jnp.dot(lhs, rhs, preferred_element_type=F32)
            else:
                rhs = joined([w[:, feat(x)] for _, x in parts], 1)
                term = lax.dot_general(lhs, rhs, NT, preferred_element_type=F32)
            span = slice(n * hidden, (n + 1) * hidden)
            if j == 0:
                acc[:, span] = term
            else:
                acc[:, span] += term

    for d in range(2):
        raw_copy(1, d).start()

    square = lax.broadcasted_iota(jnp.int32, (toks, toks), 0) == lax.broadcasted_iota(
        jnp.int32, (toks, toks), 1
    )

    def column_of(ref, k):
        return jnp.sum(jnp.where(square, ref[k : k + 1, :].astype(F32), 0.0), axis=1, keepdims=True)

    gate_col = [column_of(gates_ref, k) for k in range(2)]
    route_col = [column_of(routes_ref, k) for k in range(2)]
    for k in range(2):
        gate_cols[k] = jnp.broadcast_to(gate_col[k], (toks, cols))
    lane = lax.broadcasted_iota(jnp.int32, (toks, 128), 1)
    chosen = [(route_col[k] == lane.astype(F32)).astype(F32) for k in range(2)]
    before = (
        lax.broadcasted_iota(jnp.int32, (toks, toks), 1) < lax.broadcasted_iota(jnp.int32, (toks, toks), 0)
    ).astype(BF16)
    counts = jnp.dot(before, (chosen[0] + chosen[1]).astype(BF16), preferred_element_type=F32)
    target = [
        jnp.sum(chosen[k] * (counts + (lane * pair).astype(F32)), axis=1, keepdims=True) for k in range(2)
    ]
    wide = lax.broadcasted_iota(jnp.int32, (toks, rows), 1).astype(F32)
    for k in range(2):
        pick_ref[k * toks : (k + 1) * toks, :] = (wide == target[k]).astype(BF16)
    pick_ref[2 * toks : 3 * toks, :] = (
        (wide == target[0] + cap).astype(F32) + (wide == target[1] + cap).astype(F32)
    ).astype(BF16)
    token = lax.broadcasted_iota(jnp.int32, (toks, 2 * toks), 0)
    column = lax.broadcasted_iota(jnp.int32, (toks, 2 * toks), 1)
    diagonal = (column == token) | (column == token + toks)
    down_rows = lax.broadcasted_iota(jnp.int32, (rows, 2 * toks), 0).astype(F32)
    lanes1 = lax.broadcasted_iota(jnp.int32, (1, 2 * toks), 1)
    second = jnp.where(lanes1 < toks, 0.0, float(cap))
    placing, scale = 0.0, 0.0
    for k in range(2):
        row_target = jnp.sum(jnp.where(diagonal, target[k], 0.0), axis=0, keepdims=True) + second
        row_gate = jnp.sum(jnp.where(diagonal, gate_col[k], 0.0), axis=0, keepdims=True)
        row_gate = jnp.where(lanes1 < toks, 1.0, row_gate)
        hit = down_rows == row_target
        placing = placing + hit.astype(F32)
        scale = scale + jnp.sum(jnp.where(hit, row_gate, 0.0), axis=1, keepdims=True)
    qt_ref[...] = placing.astype(BF16)
    gs_ref[...] = jnp.broadcast_to(scale, (rows, 128))

    dispatch(0)
    for j in range(1, last + 1):
        for d in range(2):
            raw_copy(j, d).wait_recv()
            if j < last:
                raw_copy(j + 1, d).start()
            else:
                far_copy(d).start()
            fill_copy(j, d).start()
            if j in OUTER:
                outer_copy(j, d).start()
        if j > 1:
            for d in range(2):
                fill_copy(j - 1, d).wait_recv()
                if j - 1 in OUTER:
                    outer_copy(j - 1, d).wait_recv()
        dispatch(j)
        pass_on(j - 1)
        if j == 1:
            for load in loads:
                load.wait()
        accumulate(j - 1, j - 3)
        for d in range(2):
            raw_copy(j, d).wait_send()
    for d in range(2):
        fill_copy(last, d).wait_recv()
        far_copy(d).wait_recv()
    dispatch(last + 1)
    pass_on(last)
    accumulate(last, last - 2)
    pass_on(last + 1)
    accumulate(last + 1, last - 1)

    for j in range(ne // 2):
        top = 2 * pair * j
        mine = jnp.concatenate([acc[top : top + cap, :], acc[top + pair : top + pair + cap, :]], axis=0)
        gh = jnp.concatenate(
            [acc[top + cap : top + pair, 2 * hidden :], acc[top + pair + cap : top + 2 * pair, 2 * hidden :]],
            axis=0,
        )
        gate, up = mine[:, :hidden], mine[:, hidden : 2 * hidden]
        sigmoid = jax.nn.sigmoid(gate)
        active = gate * sigmoid
        span = slice(pair * j, pair * (j + 1))
        hid[span, :] = (active * up).astype(BF16)
        gg[span, :] = (gh * up * sigmoid * (1.0 + gate * (1.0 - sigmoid))).astype(BF16)
        gu[span, :] = (gh * active).astype(BF16)

    def partial(offsets):
        down = joined([wd[:, feat(o)] for o in offsets], 1)
        gate = joined([wg[feat(o), :] for o in offsets], 0)
        up = joined([wu[feat(o), :] for o in offsets], 0)
        out = jnp.dot(hid[...], down, preferred_element_type=F32)
        grad = lax.dot_general(gg[...], gate, NT, preferred_element_type=F32)
        grad = grad + lax.dot_general(gu[...], up, NT, preferred_element_type=F32)
        parts = []
        for e in range(ne):
            parts += [out[cap * e : cap * (e + 1)], grad[cap * e : cap * (e + 1)]]
        both = jnp.concatenate(parts, axis=0)
        return [both[:, s * cols : (s + 1) * cols] for s in range(len(offsets))]

    def po_copy(j, d):
        i = 2 * j + d
        return remote(odd_out.at[j, d], odd_in.at[j, d], po_s.at[i], po_r.at[i], at_z(2 * d - 1))

    def send_odd(j):
        if j in OUTER:
            return
        for d, block in enumerate(partial([-hop * j - 1, hop * j + 1])):
            odd_out[j, d] = block.astype(BF16)
            po_copy(j, d).start()

    def send_group(j):
        a, n = places(j)
        total = partial([offset(j, s) for s in range(a, a + n)])
        if j < last and j not in OUTER:
            for d in range(2):
                po_copy(j, d).wait_recv()
                to = 0 if j == 0 else d
                total[to] = total[to] + odd_in[j, d].astype(F32)
        for s in range(n):
            back[j, :, a + s] = total[s].astype(BF16).reshape(ne, pair, cols)
        exchange(j, back, home, b_s, b_r)

    def back_fill(j, d):
        i = 2 * (j - 1) + d
        return remote(fill_out.at[j, d], fill_in.at[j, d], f_s.at[i], f_r.at[i], at_z(1 - 2 * d))

    def back_outer(j, d):
        i = 2 * last + 2 + 2 * j + d
        return remote(fill_out.at[j, 2 + d], fill_in.at[j, 2 + d], f_s.at[i], f_r.at[i], at_z(2 * d - 1))

    def back_far(d):
        i = 2 * last + d
        part = pl.ds(d * toks, toks)
        return remote(fill_out.at[0, 0, part], far_in.at[part], f_s.at[i], f_r.at[i], at_z(2 * d - 1))

    def chain_copy(j, d):
        i = 2 * (j - 1) + d
        return remote(chain_out.at[j, d], chain_in.at[j - 1, d], c_s.at[i], c_r.at[i], at_z(2 * hop * d - hop))

    def combine(j):
        a, n = places(j)
        exchanged(j, home, b_s, b_r).wait_recv()
        block = joined([home[j, s].reshape(rows, cols) for s in range(a, a + n)], 1)
        picked = jnp.dot(pick_ref[...], block, preferred_element_type=F32)
        sums = [None] * 6
        for s in range(n):
            one = picked[:, s * cols : (s + 1) * cols]
            mixed = gate_cols[0] * one[:toks] + gate_cols[1] * one[toks : 2 * toks]
            sums[a + s] = jnp.concatenate([mixed, one[2 * toks :]], axis=0)
        if j > 1:
            for d in range(2):
                fill_out[j - 1, d] = sums[2 + d].astype(BF16)
                back_fill(j - 1, d).start()
                if j - 1 in OUTER and j <= last:
                    fill_out[j - 1, 2 + d] = sums[4 + d].astype(BF16)
                    back_outer(j - 1, d).start()
        if j == last + 1:
            fill_out[0, 0] = sums[1].astype(BF16)
            for d in range(2):
                back_far(d).start()
        return sums

    def chain_step(j):
        sums = combine(j)
        for d in range(2):
            back_fill(j, d).wait_recv()
            total = sums[d] + fill_in[j, d].astype(F32)
            if j in OUTER:
                back_outer(j, d).wait_recv()
                total = total + fill_in[j, 2 + d].astype(F32)
            if j == last:
                back_far(d).wait_recv()
                half = far_in[d * toks : (d + 1) * toks, :].astype(F32)
                none = jnp.zeros_like(half)
                total = total + jnp.concatenate([half, none] if d == 0 else [none, half], axis=0)
            else:
                chain_copy(j + 1, d).wait_recv()
                total = total + chain_in[j, d].astype(F32)
            chain_out[j, d] = total.astype(BF16)
            chain_copy(j, d).start()

    send_group(last + 1)
    send_odd(last - 1)
    send_group(last)
    send_odd(last - 2)
    combine(last + 1)
    send_group(last - 1)
    send_odd(last - 3)
    chain_step(last)
    for j in range(last - 2, 0, -1):
        send_group(j)
        if j > 1:
            send_odd(j - 2)
        chain_step(j + 1)
    send_group(0)
    chain_step(1)
    sums = combine(0)[0]
    for d in range(2):
        for j in range(1, last + 1):
            fill_copy(j, d).wait_send()
            back_fill(j, d).wait_send()
            chain_copy(j, d).wait_send()
        far_copy(d).wait_send()
        back_far(d).wait_send()
        for j in range(last):
            if j in OUTER:
                outer_copy(j, d).wait_send()
                back_outer(j, d).wait_send()
            else:
                odd_copy(j, d).wait_send()
                po_copy(j, d).wait_send()
    for j in range(last + 2):
        exchanged(j, slots, y_s, y_r).wait_send()
        exchanged(j, home, b_s, b_r).wait_send()
    for d in range(2):
        chain_copy(1, d).wait_recv()
        sums = sums + chain_in[0, d].astype(F32)
    out_ref[0] = sums[:toks].astype(BF16)
    out_ref[1] = sums[toks:].astype(BF16)


def shards(tokens, cotangent, routes, gates, w_gate, w_up, w_down):
    ne, nz = lax.axis_size("expert"), lax.axis_size("tensor")
    toks, cols = tokens.shape
    width, hidden = w_gate.shape[1:]
    cap = toks * routes.shape[1] * 3 // (2 * ne)
    pair = 2 * cap
    rows = ne * pair
    last = (nz // 2 - 1) // 3
    groups = last + 2
    vmem = pl.BlockSpec(memory_space=pltpu.VMEM)
    hbm = pl.BlockSpec(memory_space=pl.ANY)
    dma = pltpu.SemaphoreType.DMA
    out = jax.ShapeDtypeStruct((2, toks, cols), BF16)
    staged = pltpu.VMEM((groups, ne, 6, pair, cols), BF16)
    landed = pltpu.VMEM((groups, 6, ne, pair, cols), BF16)
    flat = pltpu.VMEM((last, 2, rows, cols), BF16)
    tokens_of = pltpu.VMEM((last + 1, 4, 2 * toks, cols), BF16)
    both = pl.pallas_call(
        functools.partial(kernel, cap, nz),
        out_shape=out,
        in_specs=[hbm] * 7,
        out_specs=vmem,
        scratch_shapes=[
            pltpu.VMEM((width, hidden), BF16),
            pltpu.VMEM((width, hidden), BF16),
            pltpu.VMEM((hidden, width), BF16),
            pltpu.VMEM((groups, 6, 2 * toks, cols), BF16),
            staged,
            landed,
            pltpu.VMEM((last, 2, ne, pair, cols), BF16),
            pltpu.VMEM((rows, 3 * hidden), F32),
            pltpu.VMEM((rows // 2, hidden), BF16),
            pltpu.VMEM((rows // 2, hidden), BF16),
            pltpu.VMEM((rows // 2, hidden), BF16),
            pltpu.VMEM((rows, 2 * toks), BF16),
            pltpu.VMEM((rows, 128), F32),
            pltpu.VMEM((3 * toks, rows), BF16),
            pltpu.VMEM((2, toks), jnp.int32),
            pltpu.VMEM((2, toks), F32),
            pltpu.VMEM((2, toks, cols), F32),
            flat,
            flat,
            staged,
            landed,
            tokens_of,
            tokens_of,
            pltpu.VMEM((2 * toks, cols), BF16),
            tokens_of,
            tokens_of,
            dma((7,)),
            dma((6 * last + 2,)),
            dma((6 * last + 2,)),
            dma((groups,)),
            dma((groups,)),
            dma((2 * last,)),
            dma((2 * last,)),
            dma((2 * last,)),
            dma((2 * last,)),
            dma((groups,)),
            dma((groups,)),
            dma((4 * last + 2,)),
            dma((4 * last + 2,)),
            dma((2 * last,)),
            dma((2 * last,)),
        ],
        name="moe_layer",
        cost_estimate=pl.CostEstimate(
            flops=12 * rows * width * hidden, bytes_accessed=6 * width * hidden, transcendentals=rows * hidden
        ),
        compiler_params=pltpu.CompilerParams(
            collective_id=0, has_side_effects=True, vmem_limit_bytes=60 * 1024 * 1024
        ),
    )(tokens, cotangent, routes.T, gates.T, w_gate, w_up, w_down)
    return both[0], both[1]


def solution(mesh):
    return jax.shard_map(
        shards,
        mesh=mesh,
        in_specs=(
            P(("dp", "expert"), "tensor"),
            P(("dp", "expert"), "tensor"),
            P(("dp", "expert"), None),
            P(("dp", "expert"), None),
            P("expert", None, "tensor"),
            P("expert", None, "tensor"),
            P("expert", "tensor", None),
        ),
        out_specs=(P(("dp", "expert"), "tensor"), P(("dp", "expert"), "tensor")),
        check_vma=False,
    )
```
